32 devices in a mesh: dp: 4 (over y, core), feat: 8 (over z, x).
Axes of the slice: x: 2, y: 2, z: 4, core: 2. Of those that a mesh axis runs over, the one named last changes fastest.
Arguments:
- resid: bfloat16 [16384, 768], P(('dp', 'feat')), may hold values from -6 to 6
- segments: int32 [16, 1024], P('dp'), may hold values from 0 to 15, never falling along the last dimension, each value on 1 to 128 neighbouring positions
- keep: int32 [16384], P('dp'), may hold values from 0 to 1, as said below
- ln_gain: bfloat16 [768], replicated, may hold values from 0.5 to 1.5
- ln_bias: bfloat16 [768], replicated, may hold values from -0.625 to 0.625
- qkv_weight: bfloat16 [768, 2304], replicated, may hold values from -0.21875 to 0.21875
- qkv_bias: bfloat16 [2304], replicated
- enc_weight: float32 [768, 24576], P('dp', 'feat'), may hold values from -0.21875 to 0.21875
- enc_bias: float32 [24576], P('feat'), may hold values from -0.5 to 0
- dec_weight: float32 [24576, 768], P('feat', 'dp'), may hold values from -0.0390625 to 0.0390625
- dec_bias: float32 [768], replicated, may hold values from -4 to 4
- enc_weight_m: float32 [768, 24576], P('dp', 'feat')
- enc_weight_v: float32 [768, 24576], P('dp', 'feat')
- enc_bias_m: float32 [24576], P('feat')
- enc_bias_v: float32 [24576], P('feat')
- dec_weight_m: float32 [24576, 768], P('feat', 'dp')
- dec_weight_v: float32 [24576, 768], P('feat', 'dp')
- dec_bias_m: float32 [768], replicated
- dec_bias_v: float32 [768], replicated
Outputs:
- objective_accumulate_tally: float32 [2], replicated
- overall_derivative_length: float32 [], replicated
- feature_fire: float32 [24576], P('feat')
- enc_weight_new: float32 [768, 24576], P('dp', 'feat')
- enc_weight_m_new: float32 [768, 24576], P('dp', 'feat')
- enc_weight_v_new: float32 [768, 24576], P('dp', 'feat')
- enc_bias_new: float32 [24576], P('feat')
- enc_bias_m_new: float32 [24576], P('feat')
- enc_bias_v_new: float32 [24576], P('feat')
- dec_weight_new: float32 [24576, 768], P('feat', 'dp')
- dec_weight_m_new: float32 [24576, 768], P('feat', 'dp')
- dec_weight_v_new: float32 [24576, 768], P('feat', 'dp')
- dec_bias_new: float32 [768], replicated
- dec_bias_m_new: float32 [768], replicated
- dec_bias_v_new: float32 [768], replicated
The draws below stay inside these ranges and needn't reach their ends.
Inputs may be any that keep to these rules, and one draw needn't show every extreme that they name: `segments`: within each row of 1024 tokens the context number never falls and each context holds 1 to 128 tokens, one exactly 128. `keep`: the first token of each row is 0 and the second is 1.
All inputs are finite; a program needn't handle non-finite values.
Results may differ from the reference program's by a relative error of at most 0.0018.
Values may be sent and summed in bfloat16 or wider, within the bound.
No kernel may reach another device: no remote copies, remote signals or barrier semaphores. Data moves between devices by JAX's collectives and lax.ppermute only.
A program may use at most 256 MiB of HBM per device.

```python
import math
import jax
import jax.numpy as jnp
import numpy as np
from jax import lax

D = 768
HEADS = 12
HEAD = 64
F = 24576
ROW_LEN = 1024
CTX = 128
STEP = 10
TOKENS = 16384


def moment_draw(key, shape, factor, second):
    base = factor * 0.004 / math.sqrt(F * D)
    if second:
        spread = jnp.exp(jax.random.uniform(key, shape, jnp.float32, math.log(0.5), math.log(8.0)))
        return spread * (0.001 / 0.999) * base * base
    return jax.random.normal(key, shape, jnp.float32) * (0.1 / 0.9) * base


def draw_keep(key, part):
    key = jax.random.fold_in(key, 5)
    positions = jnp.arange(TOKENS, dtype=jnp.int32)
    limit = 300 + 650 * positions // TOKENS
    ticket = jax.random.randint(key, (TOKENS,), 0, 1000, dtype=jnp.int32)
    chosen = (ticket < limit).astype(jnp.int32)
    in_row = positions % ROW_LEN
    return jnp.where(in_row == 0, 0, jnp.where(in_row == 1, 1, chosen)).astype(jnp.int32)


def draw_qkv_bias(key, part):
    key = jax.random.fold_in(key, 7)
    column = jnp.arange(3 * D, dtype=jnp.int32)
    scale = jnp.where(column < 2 * D, 0.5, 0.02).astype(jnp.float32)
    sample = jnp.clip(jax.random.normal(key, (3 * D,), jnp.float32), -6.0, 6.0)
    return (sample * scale).astype(jnp.bfloat16)


def draw_enc_weight_m(key, part):
    key = jax.random.fold_in(key, 11)
    return moment_draw(key, (D, F), 0.06 * math.sqrt(D / F), False)


def draw_enc_weight_v(key, part):
    key = jax.random.fold_in(key, 12)
    return moment_draw(key, (D, F), 0.06 * math.sqrt(D / F), True)


def draw_enc_bias_m(key, part):
    key = jax.random.fold_in(key, 13)
    return moment_draw(key, (F,), 0.7 * math.sqrt(D / F), False)


def draw_enc_bias_v(key, part):
    key = jax.random.fold_in(key, 14)
    return moment_draw(key, (F,), 0.7 * math.sqrt(D / F), True)


def draw_dec_weight_m(key, part):
    key = jax.random.fold_in(key, 15)
    return moment_draw(key, (F, D), 1.0, False)


def draw_dec_weight_v(key, part):
    key = jax.random.fold_in(key, 16)
    return moment_draw(key, (F, D), 1.0, True)


def draw_dec_bias_m(key, part):
    key = jax.random.fold_in(key, 17)
    return moment_draw(key, (D,), 1.7, False)


def draw_dec_bias_v(key, part):
    key = jax.random.fold_in(key, 18)
    return moment_draw(key, (D,), 1.7, True)


def level_of(stream_key, extent, cuts, least, top_value):
    def one(position, shards_of):
        steps = jax.random.uniform(jax.random.fold_in(jax.random.fold_in(stream_key, 6), position), (shards_of,), jnp.float32, least / len(cuts), top_value / len(cuts))
        return jnp.repeat(jnp.exp(steps), extent[position] // shards_of).reshape((-1,) + (1,) * (len(extent) - position - 1))

    loudness = one(*cuts[0])
    for cut in cuts[1:]:
        loudness = loudness * one(*cut)
    return loudness


def profile(count, total, bound, skew):
    portions = [(1 << 20) // math.isqrt(rank ** skew) + 1 for rank in range(2, count + 1)]
    rest, counts = total - bound - (count - 1), [1] * (count - 1)
    while rest > 0:
        free = [i for i in range(count - 1) if counts[i] < bound]
        mass, remaining = sum([portions[i] for i in free]), rest
        for i in free:
            addition = min(bound - counts[i], max(1, remaining * portions[i] // mass), rest)
            counts[i] = counts[i] + addition
            rest = rest - addition
    return np.array([bound] + counts)


def uneven(rng, number_of, total, most, slope):
    if number_of == 2:
        one = jax.random.randint(rng, (), max(1, total - most), min(most, total - 1) + 1)
        return jnp.stack([one, total - one])
    tallies = jnp.asarray(profile(number_of, total, most, slope), jnp.int32)
    pairs = (number_of - 1) // 2
    donor, taker = tallies[1:1 + 2 * pairs:2], tallies[2:2 + 2 * pairs:2]
    room = jnp.minimum(donor - 1, most - taker)
    passed = jax.random.randint(jax.random.fold_in(rng, 1), (pairs,), 0, 1 << 20) % (room + 1)
    tallies = tallies.at[1:1 + 2 * pairs:2].set(donor - passed).at[2:2 + 2 * pairs:2].set(taker + passed)
    return tallies[jax.random.permutation(jax.random.fold_in(rng, 2), number_of)]


def gaussian(own_key, shape, scale, most, shards=(), kind=jnp.bfloat16):
    array = jax.random.normal(own_key, shape, jnp.float32) * scale
    if len(shards) > 0:
        array = level_of(own_key, shape, shards, -0.22, 0.18) * array
    return jnp.clip(array, min=-most, max=most).astype(kind)


def setup_inputs(seed: int = 0) -> dict:
    key_of = jax.random.split(jax.random.key(seed), 20)
    resid = gaussian(key_of[0], (TOKENS, D), 1.0, 6.0, ((0, 32),))
    segments = jax.vmap(lambda own: jnp.searchsorted(jnp.cumsum(uneven(own, 2 * ROW_LEN // CTX, ROW_LEN, CTX, 1)), jnp.arange(ROW_LEN), side="right"))(jax.random.split(key_of[1], (TOKENS // ROW_LEN))).reshape((TOKENS // ROW_LEN, ROW_LEN)).astype(jnp.int32)
    keep = draw_keep(jax.random.fold_in(key_of[19], 71), 0)
    ln_gain = jnp.clip(1.0 + 0.1 * jax.random.normal(key_of[3], (D,), jnp.float32), 0.5, 1.5).astype(jnp.bfloat16)
    ln_bias = gaussian(key_of[4], (D,), 0.04, 0.625)
    qkv_weight = gaussian(key_of[5], (D, 3 * D), D ** -0.5, 0.21875)
    qkv_bias = draw_qkv_bias(jax.random.fold_in(key_of[19], 71), 0)
    enc_weight = gaussian(key_of[7], (D, F), D ** -0.5, 0.21875, ((0, 4), (1, 8)), jnp.float32)
    enc_bias = jnp.clip(-0.5 + 0.5 * jax.random.uniform(key_of[8], (F,), jnp.float32) ** level_of(key_of[8], (F,), ((0, 8),), -0.2, 0.2), -0.5, 0.0)
    dec_weight = gaussian(key_of[9], (F, D), F ** -0.5, 0.0390625, ((0, 8), (1, 4)), jnp.float32)
    dec_bias = gaussian(key_of[10], (D,), 0.3, 4.0, (), jnp.float32)
    enc_weight_m = draw_enc_weight_m(jax.random.fold_in(key_of[19], 71), 0)
    enc_weight_v = draw_enc_weight_v(jax.random.fold_in(key_of[19], 71), 0)
    enc_bias_m = draw_enc_bias_m(jax.random.fold_in(key_of[19], 71), 0)
    enc_bias_v = draw_enc_bias_v(jax.random.fold_in(key_of[19], 71), 0)
    dec_weight_m = draw_dec_weight_m(jax.random.fold_in(key_of[19], 71), 0)
    dec_weight_v = draw_dec_weight_v(jax.random.fold_in(key_of[19], 71), 0)
    dec_bias_m = draw_dec_bias_m(jax.random.fold_in(key_of[19], 71), 0)
    dec_bias_v = draw_dec_bias_v(jax.random.fold_in(key_of[19], 71), 0)
    return dict(resid=resid, segments=segments, keep=keep, ln_gain=ln_gain, ln_bias=ln_bias, qkv_weight=qkv_weight, qkv_bias=qkv_bias, enc_weight=enc_weight, enc_bias=enc_bias, dec_weight=dec_weight, dec_bias=dec_bias, enc_weight_m=enc_weight_m, enc_weight_v=enc_weight_v, enc_bias_m=enc_bias_m, enc_bias_v=enc_bias_v, dec_weight_m=dec_weight_m, dec_weight_v=dec_weight_v, dec_bias_m=dec_bias_m, dec_bias_v=dec_bias_v)


STRICT_ARITHMETIC = lax.Precision.HIGHEST
LAMBDA = 0.001
CLIP_NORM = 0.004
LEARN = 0.02
BETA_ONE = 0.9
BETA_TWO = 0.999
EPSILON = 1e-08
DECAY = 0.01

@jax.custom_vjp
def low(v):
    return lax.optimization_barrier(v.astype(jnp.bfloat16)).astype(jnp.float32)

@jax.custom_vjp
def low_back(v):
    return v

def low_keep(v):
    return (low(v), None)

def low_pass(kept, grad):
    return (grad,)

def back_keep(v):
    return (v, None)

def back_low(kept, grad):
    return (low(grad),)
low.defvjp(low_keep, low_pass)
low_back.defvjp(back_keep, back_low)

def attend_row(inputs, ln_gain, ln_bias, qkv_weight, qkv_bias):
    row_resid, seg_row = inputs
    values_in = row_resid.astype(jnp.float32)
    average = lax.optimization_barrier(jnp.mean(values_in, axis=1, keepdims=True))
    centred = values_in - average
    variance = lax.optimization_barrier(jnp.mean(centred * centred, axis=1, keepdims=True))
    normed = low(centred * lax.rsqrt(variance + 1e-05) * ln_gain + ln_bias)
    projected = low(jnp.dot(normed, qkv_weight, precision=STRICT_ARITHMETIC) + qkv_bias)
    query = projected[:, :D].reshape(ROW_LEN, HEADS, HEAD)
    keys = projected[:, D:2 * D].reshape(ROW_LEN, HEADS, HEAD)
    values = projected[:, 2 * D:].reshape(ROW_LEN, HEADS, HEAD)
    scores = jnp.einsum('qhd,khd->hqk', query, keys, precision=STRICT_ARITHMETIC) / math.sqrt(HEAD)
    places = jnp.arange(ROW_LEN, dtype=jnp.int32)
    allowed = (seg_row[:, None] == seg_row[None, :]) & (places[None, :] <= places[:, None])
    scores = jnp.where(allowed[None], scores, -1e+30)
    highest = lax.optimization_barrier(jnp.max(scores, axis=2, keepdims=True))
    expo = jnp.exp(scores - highest)
    probs = low(expo / lax.optimization_barrier(jnp.sum(expo, axis=2, keepdims=True)))
    mixed = jnp.einsum('hqk,khd->qhd', probs, values, precision=STRICT_ARITHMETIC)
    return mixed.reshape(ROW_LEN, D).astype(jnp.bfloat16)

def adamw(weight, grad, first, second, decay):
    first = BETA_ONE * first + (1.0 - BETA_ONE) * grad
    second = BETA_TWO * second + (1.0 - BETA_TWO) * grad * grad
    hat_first = first / (1.0 - BETA_ONE ** STEP)
    hat_second = second / (1.0 - BETA_TWO ** STEP)
    weight = weight - LEARN * (hat_first / (jnp.sqrt(hat_second) + EPSILON) + decay * weight)
    return (weight, first, second)

def reference(resid, segments, keep, ln_gain, ln_bias, qkv_weight, qkv_bias, enc_weight, enc_bias, dec_weight, dec_bias, enc_weight_m, enc_weight_v, enc_bias_m, enc_bias_v, dec_weight_m, dec_weight_v, dec_bias_m, dec_bias_v):
    row_total = TOKENS // ROW_LEN
    frozen = (ln_gain.astype(jnp.float32), ln_bias.astype(jnp.float32), qkv_weight.astype(jnp.float32), qkv_bias.astype(jnp.float32))
    tokens_z = lax.map(lambda inputs: attend_row(inputs, *frozen), (resid.reshape(row_total, ROW_LEN, D), segments))
    hidden_code_float32 = tokens_z.astype(jnp.float32)
    entry_retain_flags = keep.astype(jnp.float32).reshape(row_total, ROW_LEN)
    counted = jnp.sum(entry_retain_flags)
    mean_square = jnp.sum(entry_retain_flags * lax.optimization_barrier(jnp.sum(hidden_code_float32 * hidden_code_float32, axis=2))) / (counted * D) + 1e-06

    def objective_aggregate(trainable_tensors):
        enc_w, enc_b, dec_w, dec_b = trainable_tensors
        enc_low = low(enc_w)
        dec_low = low(dec_w)
        row_norm = jnp.sqrt(lax.optimization_barrier(jnp.sum(dec_low * dec_low, axis=1)))

        def sequence_piece(evolving_state, inputs):
            z_block, segment_retain_flags = inputs
            preact = low_back(jnp.dot(z_block, enc_low, precision=STRICT_ARITHMETIC)) + enc_b
            dictionary_response = jax.nn.softplus(preact)
            recon = low_back(jnp.dot(low(dictionary_response), dec_low, precision=STRICT_ARITHMETIC)) + dec_b
            residue = recon - z_block
            position_errors = lax.optimization_barrier(jnp.sum(residue * residue, axis=1)) / (D * mean_square) + LAMBDA * jnp.dot(dictionary_response, row_norm, precision=STRICT_ARITHMETIC)
            nonzero_tallies = jnp.dot(segment_retain_flags, jnp.tanh(dictionary_response), precision=STRICT_ARITHMETIC)
            return ((evolving_state[0] + jnp.sum(segment_retain_flags * position_errors), evolving_state[1] + nonzero_tallies), None)
        starting_state = (jnp.zeros((), jnp.float32), jnp.zeros((F,), jnp.float32))
        (accumulated_entries, nonzero_tallies), discarded_output = lax.scan(jax.checkpoint(sequence_piece), starting_state, (hidden_code_float32, entry_retain_flags))
        return (accumulated_entries, nonzero_tallies)
    trainable_tensors = (enc_weight, enc_bias, dec_weight, dec_bias)
    accumulated_entries, reverse_derivative_rule, nonzero_tallies = jax.vjp(objective_aggregate, trainable_tensors, has_aux=True)
    grads, = reverse_derivative_rule(jnp.asarray(1.0, jnp.float32) / counted)
    enc_grad, intake_offset_derivative, dec_grad, dec_bias_grad = grads
    squares = jnp.sum(enc_grad * enc_grad) + jnp.sum(intake_offset_derivative * intake_offset_derivative) + jnp.sum(dec_grad * dec_grad) + jnp.sum(dec_bias_grad * dec_bias_grad)
    overall_derivative_length = jnp.sqrt(squares)
    factor = jnp.minimum(1.0, CLIP_NORM / (overall_derivative_length + 1e-06))
    intake_matrix_revised, intake_matrix_mean_estimate, intake_matrix_square_estimate = adamw(enc_weight, enc_grad * factor, enc_weight_m, enc_weight_v, DECAY)
    intake_offset_revised, intake_offset_mean_estimate, intake_offset_square_estimate = adamw(enc_bias, intake_offset_derivative * factor, enc_bias_m, enc_bias_v, 0.0)
    readout_matrix_revised, readout_matrix_mean_estimate, readout_matrix_square_estimate = adamw(dec_weight, dec_grad * factor, dec_weight_m, dec_weight_v, DECAY)
    readout_offset_revised, readout_offset_mean_estimate, readout_offset_square_estimate = adamw(dec_bias, dec_bias_grad * factor, dec_bias_m, dec_bias_v, 0.0)
    readout_matrix_revised = readout_matrix_revised * lax.rsqrt(lax.optimization_barrier(jnp.sum(readout_matrix_revised * readout_matrix_revised, axis=1, keepdims=True)) + 1e-12)
    objective_accumulate_tally = jnp.stack([accumulated_entries, counted])
    return (objective_accumulate_tally, overall_derivative_length, nonzero_tallies, intake_matrix_revised, intake_matrix_mean_estimate, intake_matrix_square_estimate, intake_offset_revised, intake_offset_mean_estimate, intake_offset_square_estimate, readout_matrix_revised, readout_matrix_mean_estimate, readout_matrix_square_estimate, readout_offset_revised, readout_offset_mean_estimate, readout_offset_square_estimate)
```

```python
import functools
import math

import jax
import jax.numpy as jnp
from jax import lax
from jax.experimental import pallas as pl
from jax.experimental.pallas import tpu as pltpu
from jax.sharding import PartitionSpec as P

HEAD = 64
ROW_LEN = 1024
CTX = 128
STEP = 10

LAMBDA = 0.001
CLIP_NORM = 0.004
LEARN = 0.02
BETA_ONE = 0.9
BETA_TWO = 0.999
EPSILON = 1e-08
DECAY = 0.01

FEATURE_BLOCK = 512
ROW_BLOCK = 256
LAST_PARTS = 3
VMEM_BYTES = 56 * 2**20
BF16 = jnp.bfloat16
F32 = jnp.float32


def kernel_params():
    return pltpu.CompilerParams(vmem_limit_bytes=VMEM_BYTES)


def dot_nn(a, b):
    return jnp.dot(a, b, preferred_element_type=F32)


def dot_nt(a, b):
    return lax.dot_general(a, b, (((1,), (1,)), ((), ())), preferred_element_type=F32)


def attend_kernel(own_ref, tail_ref, seg_q_ref, seg_k_ref, gain_ref, bias_ref, w_ref, wb_ref, z_ref, q_s, kv_s):
    rows, width = own_ref.shape

    def normed(block):
        values = block.astype(F32)
        centred = values - jnp.mean(values, axis=1, keepdims=True)
        variance = jnp.mean(centred * centred, axis=1, keepdims=True)
        gain = gain_ref[...].astype(F32)
        return (centred * lax.rsqrt(variance + 1e-05) * gain + bias_ref[...].astype(F32)).astype(BF16)

    own = normed(own_ref[...])
    q_s[...] = (dot_nn(own, w_ref[:, :width]) + wb_ref[:, :width].astype(F32)).astype(BF16)
    kv_s[CTX:, :] = (dot_nn(own, w_ref[:, width:]) + wb_ref[:, width:].astype(F32)).astype(BF16)
    tail = normed(tail_ref[...])
    kv_s[:CTX, :] = (dot_nn(tail, w_ref[:, width:]) + wb_ref[:, width:].astype(F32)).astype(BF16)

    lane = lax.broadcasted_iota(jnp.int32, (CTX, 2 * HEAD), 1)
    first_head = lane < HEAD
    for block in range(rows // CTX):
        base = block * CTX
        place_q = lax.broadcasted_iota(jnp.int32, (CTX, 2 * CTX), 0) + CTX
        place_k = lax.broadcasted_iota(jnp.int32, (CTX, 2 * CTX), 1)
        allowed = (seg_q_ref[base : base + CTX, :] == seg_k_ref[:, base : base + 2 * CTX]) & (place_k <= place_q)
        for pair in range(width // (2 * HEAD)):
            columns = slice(pair * 2 * HEAD, (pair + 1) * 2 * HEAD)
            query = q_s[base : base + CTX, columns]
            keys = kv_s[base : base + 2 * CTX, columns]
            values = kv_s[base : base + 2 * CTX, width + pair * 2 * HEAD : width + (pair + 1) * 2 * HEAD]
            mixed = []
            for half in range(2):
                mine = first_head if half == 0 else ~first_head
                part = jnp.where(mine, query, jnp.zeros_like(query))
                scores = dot_nt(part, keys) * (1.0 / math.sqrt(HEAD))
                scores = jnp.where(allowed, scores, -1e30)
                expo = jnp.exp(scores - jnp.max(scores, axis=1, keepdims=True))
                probs = (expo / jnp.sum(expo, axis=1, keepdims=True)).astype(BF16)
                mixed.append(dot_nn(probs, values))
            z_ref[base : base + CTX, columns] = jnp.where(first_head, mixed[0], mixed[1]).astype(BF16)


def attend(resid, tail, seg_q, seg_k, ln_gain, ln_bias, qkv_weight, qkv_bias):
    rows, width = resid.shape
    return pl.pallas_call(
        attend_kernel,
        out_shape=jax.ShapeDtypeStruct((rows, width), BF16),
        scratch_shapes=[
            pltpu.VMEM((rows, width), BF16),
            pltpu.VMEM((rows + CTX, 2 * width), BF16),
        ],
        compiler_params=kernel_params(),
        cost_estimate=pl.CostEstimate(flops=8 * rows * width * width, bytes_accessed=2 * 3 * width * width, transcendentals=rows * 2 * CTX * 12),
        name="attend",
    )(resid, tail, seg_q, seg_k, ln_gain[None], ln_bias[None], qkv_weight, qkv_bias[None])


def encode_kernel(count, *refs):
    z_refs, (keep_ref, enc_ref, bias_ref, dec_ref), rest = refs[:count], refs[count : count + 4], refs[count + 4 :]
    act_ref, rec_refs, (sum_ref, fire_ref) = rest[0], rest[1 : 1 + count], rest[1 + count : 3 + count]
    totals = rest[3 + count :]
    step, last = pl.program_id(0), pl.num_programs(0) - 1
    features = enc_ref.shape[1]

    @pl.when(step == 0)
    def _():
        for total in totals:
            total[...] = jnp.zeros_like(total)

    sums = jnp.zeros((8, features), F32)
    fires = jnp.zeros((8, features), F32)
    start = 0
    for piece in range(count):
        block = min(ROW_BLOCK, z_refs[piece].shape[0])
        for base in range(0, z_refs[piece].shape[0], block):
            rows = slice(base, base + block)
            spot = slice(start + base, start + base + block)
            preact = dot_nn(z_refs[piece][rows, :], enc_ref[...]) + bias_ref[...]
            tiny = jnp.exp(-jnp.abs(preact))
            log_part = jnp.where(tiny < 2.0**-10, tiny * (1.0 - 0.5 * tiny), jnp.log(1.0 + tiny))
            act = jnp.maximum(preact, 0.0) + log_part
            low = act.astype(BF16)
            act_ref[spot, :] = low
            kept = keep_ref[spot, :]
            sums = sums + jnp.sum((kept * act).reshape(block // 8, 8, features), axis=0)
            fires = fires + jnp.sum((kept * jnp.tanh(act)).reshape(block // 8, 8, features), axis=0)
            part = dot_nt(low, dec_ref[...])
            totals[piece][rows, :] += part
        start += z_refs[piece].shape[0]
    sum_ref[...] = jnp.sum(sums, axis=0, keepdims=True)
    fire_ref[...] = jnp.sum(fires, axis=0, keepdims=True)

    @pl.when(step == last)
    def _():
        for piece in range(count):
            rec_refs[piece][...] = totals[piece][...].astype(rec_refs[piece].dtype)


def encode(pieces, keep_column, enc, bias, dec_t, out_dtype):
    width, features = enc.shape
    sizes = [p.shape[0] for p in pieces]
    tokens = sum(sizes)
    fb = FEATURE_BLOCK
    whole = lambda j: (0, 0)
    across = lambda j: (0, j)
    outs = pl.pallas_call(
        functools.partial(encode_kernel, len(pieces)),
        grid=(features // fb,),
        in_specs=[pl.BlockSpec((s, width), whole) for s in sizes]
        + [
            pl.BlockSpec((tokens, 1), whole),
            pl.BlockSpec((width, fb), across),
            pl.BlockSpec((1, fb), across),
            pl.BlockSpec((width, fb), across),
        ],
        out_specs=[pl.BlockSpec((tokens, fb), across)]
        + [pl.BlockSpec((s, width), whole) for s in sizes]
        + [pl.BlockSpec((1, fb), across)] * 2,
        out_shape=[jax.ShapeDtypeStruct((tokens, features), BF16)]
        + [jax.ShapeDtypeStruct((s, width), out_dtype) for s in sizes]
        + [jax.ShapeDtypeStruct((1, features), F32)] * 2,
        scratch_shapes=[pltpu.VMEM((s, width), F32) for s in sizes],
        compiler_params=kernel_params(),
        cost_estimate=pl.CostEstimate(
            flops=4 * tokens * width * features,
            bytes_accessed=2 * (2 * width * features + tokens * (features + 4 * width)),
            transcendentals=3 * tokens * features,
        ),
        name="encode",
    )(*pieces, keep_column, enc, bias, dec_t)
    return outs[0], outs[1 : 1 + len(pieces)], outs[-2], outs[-1]


def backward_kernel(groups, carried, parted, *refs):
    refs = list(refs)
    slots = refs.pop(0) if parted else None
    acts, zs, gs = [], [], []
    for count in groups:
        acts.append(refs.pop(0))
        zs.append([refs.pop(0) for _ in range(count)])
        gs.append([refs.pop(0) for _ in range(count)])
    keep_ref, norm_ref, dec_ref = refs.pop(0), refs.pop(0), refs.pop(0)
    enc_in, dec_in = (refs.pop(0), refs.pop(0)) if carried else (None, None)
    outs = [refs.pop(0) for _ in range(4 if parted else 2)]
    bias_ref = refs.pop(0)
    z_t, g_t, pre_s = refs

    @pl.when(pl.program_id(0) == 0)
    def _():
        spot = 0
        for z_list, g_list in zip(zs, gs):
            for z_ref, g_ref in zip(z_list, g_list):
                size = z_ref.shape[0]
                z_t[:, spot : spot + size] = z_ref[...].T
                g_t[:, spot : spot + size] = g_ref[...].T
                spot += size

    features = dec_ref.shape[1]
    spot = 0
    sums = jnp.zeros((8, features), F32)
    for act_ref, g_list in zip(acts, gs):
        at = 0
        for g_ref in g_list:
            block = min(ROW_BLOCK, g_ref.shape[0])
            for base in range(0, g_ref.shape[0], block):
                grad_act = dot_nn(g_ref[base : base + block, :], dec_ref[...])
                act = act_ref[at : at + block, :].astype(F32)
                slope = jnp.where(act < 2.0**-10, act * (1.0 - 0.5 * act), 1.0 - jnp.exp(-act))
                pre = (grad_act + keep_ref[spot : spot + block, :] * norm_ref[...]) * slope
                sums = sums + jnp.sum(pre.reshape(block // 8, 8, features), axis=0)
                pre_s[spot : spot + block, :] = pre.astype(BF16)
                at += block
                spot += block
    bias_ref[...] = jnp.sum(sums, axis=0, keepdims=True)
    enc_part = dot_nn(z_t[...], pre_s[...])
    dec_part = None
    spot = 0
    for act_ref in acts:
        size = act_ref.shape[0]
        term = dot_nn(g_t[:, spot : spot + size], act_ref[...])
        dec_part = term if dec_part is None else dec_part + term
        spot += size
    if carried:
        enc_part = enc_part + enc_in[...]
        dec_part = dec_part + dec_in[...]
    if not parted:
        outs[0][...] = enc_part
        outs[1][...] = dec_part
        return
    for value, keep_out, send_out in ((enc_part, outs[0], outs[1]), (dec_part, outs[2], outs[3])):
        rows = value.shape[0] // parted
        me = slots[0]
        for owner in range(parted):
            away = owner ^ me
            half = away // 2
            piece = value[owner * rows : (owner + 1) * rows, :]

            @pl.when(away % 2 == 0)
            def _():
                keep_out[pl.ds(half, 1)] = piece[None].astype(keep_out.dtype)

            @pl.when(away % 2 == 1)
            def _():
                send_out[pl.ds(half, 1)] = piece[None].astype(send_out.dtype)


def backward(groups, keep_column, norm_scaled, dec_t, carried, first, wide, parted, me):
    width = dec_t.shape[0]
    counts = [len(zs) for _, zs, _ in groups]
    tokens = sum(act.shape[0] for act, _, _ in groups)
    fb = FEATURE_BLOCK
    start = first // fb
    whole = lambda j, *_: (0, 0)
    across = lambda j, *_: (0, j + start)
    local = lambda j, *_: (0, j)
    operands, specs = [], []
    for act, zs, gs in groups:
        operands.append(act)
        specs.append(pl.BlockSpec((act.shape[0], fb), across))
        for piece in (*zs, *gs):
            operands.append(piece)
            specs.append(pl.BlockSpec(piece.shape, whole))
    operands += [keep_column, norm_scaled, dec_t]
    specs += [pl.BlockSpec((tokens, 1), whole), pl.BlockSpec((1, fb), across), pl.BlockSpec((width, fb), across)]
    if carried is not None:
        operands += list(carried)
        specs += [pl.BlockSpec((width, fb), across)] * 2
    if parted:
        shape = (parted // 2, width // parted, wide)
        block = pl.BlockSpec((parted // 2, width // parted, fb), lambda j, *_: (0, 0, j))
        out_shape = [jax.ShapeDtypeStruct(shape, F32)] * 4
        out_specs = [block] * 4
    else:
        out_shape = [jax.ShapeDtypeStruct((width, wide), F32)] * 2
        out_specs = [pl.BlockSpec((width, fb), local)] * 2
    out_shape.append(jax.ShapeDtypeStruct((1, wide), F32))
    out_specs.append(pl.BlockSpec((1, fb), local))
    scratch = [pltpu.VMEM((width, tokens), BF16), pltpu.VMEM((width, tokens), BF16), pltpu.VMEM((tokens, fb), BF16)]
    return pl.pallas_call(
        functools.partial(backward_kernel, counts, carried is not None, parted),
        grid_spec=pltpu.PrefetchScalarGridSpec(
            num_scalar_prefetch=1 if parted else 0,
            grid=(wide // fb,),
            in_specs=specs,
            out_specs=out_specs,
            scratch_shapes=scratch,
        ),
        out_shape=out_shape,
        compiler_params=kernel_params(),
        cost_estimate=pl.CostEstimate(
            flops=6 * tokens * width * wide,
            bytes_accessed=2 * tokens * wide + 16 * width * wide,
            transcendentals=tokens * wide,
        ),
        name="backward",
    )(*([me] if parted else []), *operands)


def ring_order(count):
    return list(range(0, count, 2)) + list(range(1, count, 2))[::-1]


def ring_shift(block, direction):
    order = ring_order(lax.axis_size("feat"))
    count = len(order)
    route = [(order[i], order[(i + direction) % count]) for i in range(count)]
    return lax.ppermute(block, "feat", route)


def swapped(block, axis, bit):
    return lax.ppermute(block, axis, [(i, i ^ bit) for i in range(lax.axis_size(axis))])


def summed(block, axes):
    for axis in axes:
        bit = 1
        while bit < lax.axis_size(axis):
            block = block + swapped(block, axis, bit)
            bit *= 2
    return block


def ring_gather(own):
    half = lax.axis_size("feat") // 2
    rows = own.shape[0] // 2
    stages = [[own]]
    right, left = own, own
    for hop in range(1, half + 1):
        if hop == half:
            right, left = right[:rows], left[rows:]
        right, left = ring_shift(right, 1), ring_shift(left, -1)
        stages.append([right, left])
    return stages


def adamw(weight, grad, first, second, decay):
    first = BETA_ONE * first + (1.0 - BETA_ONE) * grad
    second = BETA_TWO * second + (1.0 - BETA_TWO) * grad * grad
    hat_first = first / (1.0 - BETA_ONE**STEP)
    hat_second = second / (1.0 - BETA_TWO**STEP)
    weight = weight - LEARN * (hat_first / (jnp.sqrt(hat_second) + EPSILON) + decay * weight)
    return (weight, first, second)


def shards(
    resid,
    segments,
    keep,
    ln_gain,
    ln_bias,
    qkv_weight,
    qkv_bias,
    enc_weight,
    enc_bias,
    dec_weight,
    dec_bias,
    enc_weight_m,
    enc_weight_v,
    enc_bias_m,
    enc_bias_v,
    dec_weight_m,
    dec_weight_v,
    dec_bias_m,
    dec_bias_v,
):
    own_rows, width = resid.shape
    group = keep.shape[0]
    feat_size, dp_size = lax.axis_size("feat"), lax.axis_size("dp")
    half = feat_size // 2
    features = enc_weight.shape[1]
    feat_at, dp_at = lax.axis_index("feat"), lax.axis_index("dp")
    everywhere = ("dp", "feat")

    tail = lax.ppermute(resid[own_rows - CTX :], "feat", [(i, i + 1) for i in range(feat_size - 1)])
    enc_full = lax.all_gather(enc_weight.astype(BF16), "dp", axis=0, tiled=True)
    dec_full = lax.all_gather(dec_weight.astype(BF16).T, "dp", axis=0, tiled=True)

    offset = feat_at * own_rows
    row_ids = jnp.arange(group, dtype=jnp.int32)
    seg_all = segments.reshape(group) + row_ids // ROW_LEN * ROW_LEN
    own_seg = lax.dynamic_slice_in_dim(seg_all, offset, own_rows)
    tail_seg = lax.dynamic_slice_in_dim(seg_all, jnp.maximum(offset - CTX, 0), CTX)
    tail_seg = jnp.where(feat_at > 0, tail_seg, -1)
    key_seg = jnp.concatenate([tail_seg, own_seg])
    tokens_z = attend(resid, tail, own_seg[:, None], key_seg[None], ln_gain, ln_bias, qkv_weight, qkv_bias)

    order = jnp.asarray(ring_order(feat_size), jnp.int32)
    place = jnp.where(feat_at % 2 == 0, feat_at // 2, feat_size - 1 - feat_at // 2)
    keep_mask = keep.astype(F32)
    keep_rows = keep_mask.reshape(feat_size, own_rows)
    hops = [0]
    for hop in range(1, half):
        hops += [-hop, hop]
    hops.append(half)
    owners = order[(place + jnp.asarray(hops, jnp.int32)) % feat_size]
    keep_ring = keep_rows[owners].reshape(group, 1)
    keep_stage = [keep_ring[:own_rows]]
    for hop in range(1, half):
        keep_stage.append(keep_ring[(2 * hop - 1) * own_rows : (2 * hop + 1) * own_rows])
    keep_stage.append(keep_ring[group - own_rows :])
    own_keep = keep_stage[0]

    z_float = tokens_z.astype(F32)
    counted, squares = summed(
        jnp.stack([jnp.sum(own_keep), jnp.sum(own_keep * z_float * z_float)]), everywhere
    )
    mean_square = squares / (counted * width) + 1e-06
    unit = 2.0 / (width * mean_square * counted)

    z_stages = ring_gather(tokens_z)
    row_norm = jnp.sqrt(jnp.sum(dec_full.astype(F32) ** 2, axis=0, keepdims=True))
    acts, recs, sums, fires = [], [], [], []
    for hop, pieces in enumerate(z_stages):
        act, rec, act_sum, fire = encode(
            pieces, keep_stage[hop], enc_full, enc_bias[None], dec_full, BF16 if hop == half else F32
        )
        acts.append(act)
        recs.append(rec)
        sums.append(act_sum)
        fires.append(fire)
    act_sum, fire_sum = sum(sums), sum(fires)

    rows = own_rows // 2
    right, left = recs[half]
    for hop in range(half - 1, -1, -1):
        right, left = ring_shift(right, 1).astype(F32), ring_shift(left, -1).astype(F32)
        if hop == 0:
            break
        from_left, from_right = recs[hop]
        if hop == half - 1:
            right = jnp.concatenate([from_right[:rows] + right, from_right[rows:]])
            left = jnp.concatenate([from_left[:rows], from_left[rows:] + left])
        else:
            right, left = from_right + right, from_left + left
        right, left = right.astype(BF16), left.astype(BF16)
    residue = recs[0][0] + right + left + dec_bias - z_float
    grad_out = own_keep * residue * unit
    fit_part = jnp.sum(own_keep * residue * residue) / (width * mean_square)
    bias_part = jnp.sum(grad_out, axis=0)
    loss_part = fit_part + LAMBDA * jnp.sum(act_sum * row_norm)

    grad_stages = ring_gather(grad_out.astype(BF16))
    norm_scaled = LAMBDA / counted * row_norm
    me = dp_at.reshape(1).astype(jnp.int32)
    bias_grads = []
    carried = None
    plans = [[0, 1]] + [[hop] for hop in range(2, half - 1)] + [[half - 1, half]]
    for plan in plans[:-1]:
        groups = [(acts[hop], z_stages[hop], grad_stages[hop]) for hop in plan]
        keep_column = jnp.concatenate([keep_stage[hop] for hop in plan])
        *carried, bias_grad = backward(groups, keep_column, norm_scaled, dec_full, carried, 0, features, 0, None)
        bias_grads.append(bias_grad)
    plan = plans[-1]
    groups = [(acts[hop], z_stages[hop], grad_stages[hop]) for hop in plan]
    keep_column = jnp.concatenate([keep_stage[hop] for hop in plan])
    wide = features // LAST_PARTS
    enc_grads, dec_grads, last_bias = [], [], []
    for part in range(LAST_PARTS):
        enc_keep, enc_send, dec_keep, dec_send, bias_grad = backward(
            groups, keep_column, norm_scaled, dec_full, carried, part * wide, wide, dp_size, me
        )
        last_bias.append(bias_grad)
        for kept, sent, into in ((enc_keep, enc_send, enc_grads), (dec_keep, dec_send, dec_grads)):
            total = kept + swapped(sent, "dp", 1)
            own = total[0]
            for other in range(1, dp_size // 2):
                own = own + swapped(total[other].astype(BF16), "dp", 2 * other).astype(F32)
            into.append(own)
    enc_grad = jnp.concatenate(enc_grads, axis=1)
    dec_grad = jnp.concatenate(dec_grads, axis=1)
    bias_share = sum(bias_grads) + jnp.concatenate(last_bias, axis=1)
    enc_bias_grad, fired, act_total = summed(jnp.concatenate([bias_share, fire_sum, act_sum]), ("dp",))
    dec_bias_grad = summed(bias_part, everywhere)
    own_dec = dec_weight.astype(BF16).astype(F32)
    penalty = (LAMBDA / counted) * act_total / row_norm[0]
    dec_grad = dec_grad.T + penalty[:, None] * own_dec

    first_dp = dp_at == 0
    first_both = first_dp & (feat_at == 0)
    own_squares = jnp.sum(enc_grad * enc_grad) + jnp.sum(dec_grad * dec_grad)
    own_squares = own_squares + jnp.where(first_dp, jnp.sum(enc_bias_grad * enc_bias_grad), 0.0)
    own_squares = own_squares + jnp.where(first_both, jnp.sum(dec_bias_grad * dec_bias_grad), 0.0)
    total_squares, loss_total = summed(jnp.stack([own_squares, loss_part]), everywhere)
    overall_derivative_length = jnp.sqrt(total_squares)
    factor = jnp.minimum(1.0, CLIP_NORM / (overall_derivative_length + 1e-06))
    dec_new, dec_m, dec_v = adamw(dec_weight, dec_grad * factor, dec_weight_m, dec_weight_v, DECAY)
    row_squares = summed(jnp.sum(dec_new * dec_new, axis=1), ("dp",))
    enc_new, enc_m, enc_v = adamw(enc_weight, enc_grad * factor, enc_weight_m, enc_weight_v, DECAY)
    bias_new, bias_m, bias_v = adamw(enc_bias, enc_bias_grad * factor, enc_bias_m, enc_bias_v, 0.0)
    out_new, out_m, out_v = adamw(dec_bias, dec_bias_grad * factor, dec_bias_m, dec_bias_v, 0.0)
    dec_new = dec_new * lax.rsqrt(row_squares + 1e-12)[:, None]
    return (
        jnp.stack([loss_total, counted]),
        overall_derivative_length,
        fired,
        enc_new,
        enc_m,
        enc_v,
        bias_new,
        bias_m,
        bias_v,
        dec_new,
        dec_m,
        dec_v,
        out_new,
        out_m,
        out_v,
    )


def solution(mesh):
    return jax.shard_map(
        shards,
        mesh=mesh,
        in_specs=(
            P(("dp", "feat"), None),
            P("dp", None),
            P("dp"),
            P(),
            P(),
            P(),
            P(),
            P("dp", "feat"),
            P("feat"),
            P("feat", "dp"),
            P(),
            P("dp", "feat"),
            P("dp", "feat"),
            P("feat"),
            P("feat"),
            P("feat", "dp"),
            P("feat", "dp"),
            P(),
            P(),
        ),
        out_specs=(
            P(),
            P(),
            P("feat"),
            P("dp", "feat"),
            P("dp", "feat"),
            P("dp", "feat"),
            P("feat"),
            P("feat"),
            P("feat"),
            P("feat", "dp"),
            P("feat", "dp"),
            P("feat", "dp"),
            P(),
            P(),
            P(),
        ),
        check_vma=False,
    )
```

```python
import functools
import math

import jax
import jax.numpy as jnp
from jax import lax
from jax.experimental import pallas as pl
from jax.experimental.pallas import tpu as pltpu
from jax.sharding import PartitionSpec as P

HEAD = 64
ROW_LEN = 1024
CTX = 128
STEP = 10

LAMBDA = 0.001
CLIP_NORM = 0.004
LEARN = 0.02
BETA_ONE = 0.9
BETA_TWO = 0.999
EPSILON = 1e-08
DECAY = 0.01

ENCODE_BLOCK = 768
BACKWARD_BLOCK = 512
ROW_BLOCK = 512
LANES = 128
ENCODE_VMEM = 56
BACKWARD_VMEM = 56
LAST_PARTS = 3
PACK_BLOCK = 768
COST_SHARE = 4
BF16 = jnp.bfloat16
F32 = jnp.float32


def kernel_params(mebibytes):
    return pltpu.CompilerParams(vmem_limit_bytes=mebibytes * 2**20)


def dot_nn(a, b):
    return jnp.dot(a, b, preferred_element_type=F32)


def dot_nt(a, b):
    return lax.dot_general(a, b, (((1,), (1,)), ((), ())), preferred_element_type=F32)


def dot_tn(a, b):
    return lax.dot_general(a, b, (((0,), (0,)), ((), ())), preferred_element_type=F32)


def together(*values):
    leaves, tree = jax.tree.flatten(values)
    return jax.tree.unflatten(tree, lax.optimization_barrier(tuple(leaves)))


def attend_kernel(own_ref, tail_ref, seg_q_ref, seg_k_ref, gain_ref, bias_ref, w_ref, wb_ref, z_ref, q_s, kv_s):
    rows, width = own_ref.shape
    gain = gain_ref[...].astype(F32).reshape(1, width)
    shift = bias_ref[...].astype(F32).reshape(1, width)
    offsets = wb_ref[...].astype(F32).reshape(1, 3 * width)

    def normed(block):
        values = block.astype(F32)
        centred = values - jnp.mean(values, axis=1, keepdims=True)
        variance = jnp.mean(centred * centred, axis=1, keepdims=True)
        return (centred * lax.rsqrt(variance + 1e-05) * gain + shift).astype(BF16)

    own = normed(own_ref[...])
    q_s[...] = (dot_nn(own, w_ref[:, :width]) + offsets[:, :width]).astype(BF16)
    kv_s[CTX:, :] = (dot_nn(own, w_ref[:, width:]) + offsets[:, width:]).astype(BF16)
    tail = normed(tail_ref[...])
    kv_s[:CTX, :] = (dot_nn(tail, w_ref[:, width:]) + offsets[:, width:]).astype(BF16)

    lane = lax.broadcasted_iota(jnp.int32, (CTX, 2 * HEAD), 1)
    first_head = lane < HEAD
    place_q = lax.broadcasted_iota(jnp.int32, (CTX, 2 * CTX), 0) + CTX
    place_k = lax.broadcasted_iota(jnp.int32, (CTX, 2 * CTX), 1)
    earlier = place_k <= place_q
    for block in range(rows // CTX):
        base = block * CTX
        seg_q = seg_q_ref[base : base + CTX, :]
        allowed = (jnp.concatenate([seg_q, seg_q], axis=1) == seg_k_ref[:, base : base + 2 * CTX]) & earlier
        for pair in range(width // (2 * HEAD)):
            columns = slice(pair * 2 * HEAD, (pair + 1) * 2 * HEAD)
            query = q_s[base : base + CTX, columns]
            keys = kv_s[base : base + 2 * CTX, columns]
            values = kv_s[base : base + 2 * CTX, width + pair * 2 * HEAD : width + (pair + 1) * 2 * HEAD]
            mixed = []
            for half in range(2):
                mine = first_head if half == 0 else ~first_head
                part = jnp.where(mine, query, jnp.zeros_like(query))
                scores = dot_nt(part, keys) * (1.0 / math.sqrt(HEAD))
                scores = jnp.where(allowed, scores, -1e30)
                expo = jnp.exp(scores - jnp.max(scores, axis=1, keepdims=True))
                probs = (expo / jnp.sum(expo, axis=1, keepdims=True)).astype(BF16)
                mixed.append(dot_nn(probs, values))
            z_ref[base : base + CTX, columns] = jnp.where(first_head, mixed[0], mixed[1]).astype(BF16)


def attend(resid, tail, seg_q, seg_k, ln_gain, ln_bias, qkv_weight, qkv_bias):
    rows, width = resid.shape
    return pl.pallas_call(
        attend_kernel,
        out_shape=jax.ShapeDtypeStruct((rows, width), BF16),
        scratch_shapes=[
            pltpu.VMEM((rows, width), BF16),
            pltpu.VMEM((rows + CTX, 2 * width), BF16),
        ],
        compiler_params=kernel_params(32),
        cost_estimate=pl.CostEstimate(
            flops=8 * rows * width * width, bytes_accessed=6 * width * width, transcendentals=rows * 2 * CTX * 12
        ),
        name="attend",
    )(resid, tail, seg_q, seg_k, ln_gain, ln_bias, qkv_weight, qkv_bias)


def packed_kernel(enc_ref, dec_ref, out_ref):
    out_ref[0] = enc_ref[...].astype(BF16)
    out_ref[1] = dec_ref[...].astype(BF16)


def packed(enc, dec):
    rows, columns = enc.shape
    block = PACK_BLOCK
    across = lambda j: (0, j)
    return pl.pallas_call(
        packed_kernel,
        grid=(columns // block,),
        in_specs=[pl.BlockSpec((rows, block), across)] * 2,
        out_specs=pl.BlockSpec((2, rows, block), lambda j: (0, 0, j)),
        out_shape=jax.ShapeDtypeStruct((2, rows, columns), BF16),
        compiler_params=kernel_params(16),
        cost_estimate=pl.CostEstimate(flops=0, bytes_accessed=12 * rows * columns, transcendentals=0),
        name="packed",
    )(enc, dec)


def encode_kernel(count, rounded, *refs):
    z_refs, (keep_ref, enc_ref, bias_ref, dec_ref), rest = refs[:count], refs[count : count + 4], refs[count + 4 :]
    act_ref, rec_refs, (sum_ref, fire_ref, square_ref) = rest[0], rest[1 : 1 + count], rest[1 + count : 4 + count]
    totals = rest[4 + count :] if rounded else rec_refs
    step, last = pl.program_id(0), pl.num_programs(0) - 1
    features = enc_ref.shape[-1]

    def whole(ref):
        return ref[...].reshape(-1, features)

    @pl.when(step == 0)
    def _():
        spot, squares = 0, 0.0
        for total, z_ref in zip(totals, z_refs):
            total[...] = jnp.zeros_like(total)
            size, width = z_ref.shape
            values = z_ref[...].astype(F32)
            kept = wide(keep_ref[spot : spot + size, :], width) * values * values
            squares = squares + jnp.sum(kept.reshape(-1, 8, width), axis=0)
            spot += size
        square_ref[...] = jnp.sum(squares, axis=0, keepdims=True)

    blocks, spot = [], 0
    for piece in range(count):
        size = z_refs[piece].shape[0]
        block = min(ROW_BLOCK, size)
        for base in range(0, size, block):
            blocks.append((piece, slice(base, base + block), slice(spot + base, spot + base + block)))
        spot += size

    def preact_of(piece, rows):
        return dot_nn(z_refs[piece][rows, :], whole(enc_ref)) + bias_ref[...]

    sums = jnp.zeros((8, features), F32)
    fires = jnp.zeros((8, features), F32)
    coming = preact_of(*blocks[0][:2])
    for at, (piece, rows, place) in enumerate(blocks):
        preact = coming
        if at + 1 < len(blocks):
            coming = preact_of(*blocks[at + 1][:2])
        tiny = jnp.exp(-jnp.abs(preact))
        log_part = jnp.where(tiny < 2.0**-10, tiny * (1.0 - 0.5 * tiny), jnp.log(1.0 + tiny))
        act = jnp.maximum(preact, 0.0) + log_part
        low = act.astype(BF16)
        act_ref[place, :] = low
        kept = wide(keep_ref[place, :], features) * act
        sums = sums + jnp.sum(kept.reshape(-1, 8, features), axis=0)
        fires = fires + jnp.sum(jnp.tanh(kept).reshape(-1, 8, features), axis=0)
        totals[piece][rows, :] += dot_nt(low, whole(dec_ref))
    sum_ref[...] = jnp.sum(sums, axis=0, keepdims=True)
    fire_ref[...] = jnp.sum(fires, axis=0, keepdims=True)

    if rounded:

        @pl.when(step == last)
        def _():
            for piece in range(count):
                rec_refs[piece][...] = totals[piece][...].astype(BF16)


def wide(block, columns):
    return jnp.concatenate([block] * (columns // block.shape[1]), axis=1)


def encode(pieces, keep_wide, keep_at, weights, bias, rounded):
    parts, _, rows, features = weights.shape
    width = parts * rows
    sizes = [p.shape[0] for p in pieces]
    tokens = sum(sizes)
    fb = ENCODE_BLOCK
    whole = lambda j: (0, 0)
    across = lambda j: (0, j)
    keep_block = keep_at // tokens
    outs = pl.pallas_call(
        functools.partial(encode_kernel, len(pieces), rounded),
        grid=(features // fb,),
        in_specs=[pl.BlockSpec((s, width), whole) for s in sizes]
        + [
            pl.BlockSpec((tokens, LANES), lambda j: (keep_block, 0)),
            pl.BlockSpec((parts, None, rows, fb), lambda j: (0, 0, 0, j)),
            pl.BlockSpec((1, fb), across),
            pl.BlockSpec((parts, None, rows, fb), lambda j: (0, 1, 0, j)),
        ],
        out_specs=[pl.BlockSpec((tokens, fb), across)]
        + [pl.BlockSpec((s, width), whole) for s in sizes]
        + [pl.BlockSpec((1, fb), across)] * 2
        + [pl.BlockSpec((1, width), whole)],
        out_shape=[jax.ShapeDtypeStruct((tokens, features), BF16)]
        + [jax.ShapeDtypeStruct((s, width), BF16 if rounded else F32) for s in sizes]
        + [jax.ShapeDtypeStruct((1, features), F32)] * 2
        + [jax.ShapeDtypeStruct((1, width), F32)],
        scratch_shapes=[pltpu.VMEM((s, width), F32) for s in sizes] if rounded else [],
        compiler_params=kernel_params(ENCODE_VMEM),
        cost_estimate=pl.CostEstimate(
            flops=4 * tokens * width * features // COST_SHARE,
            bytes_accessed=2 * (2 * width * features + tokens * (features + 4 * width)) // COST_SHARE,
            transcendentals=3 * tokens * features // COST_SHARE,
        ),
        name="encode",
    )(*pieces, keep_wide, weights, bias, weights)
    return outs[0], outs[1 : 1 + len(pieces)], outs[-3:]


def backward_kernel(groups, carried, parted, *refs):
    refs = list(refs)
    slots = refs.pop(0) if parted else None
    acts, zs, gs, keeps = [], [], [], []
    for count in groups:
        acts.append(refs.pop(0))
        zs.append([refs.pop(0) for _ in range(count)])
        gs.append([refs.pop(0) for _ in range(count)])
        keeps.append(refs.pop(0))
    norm_ref, dec_ref = refs.pop(0), refs.pop(0)
    enc_in, dec_in = (refs.pop(0), refs.pop(0)) if carried else (None, None)
    outs = [refs.pop(0) for _ in range(2)]
    bias_ref, out_bias_ref, pre_s = refs
    features = dec_ref.shape[-1]

    @pl.when(pl.program_id(0) == 0)
    def _():
        total = 0.0
        for g_list in gs:
            for g_ref in g_list:
                total = total + jnp.sum(g_ref[...].astype(F32).reshape(-1, 8, g_ref.shape[1]), axis=0)
        out_bias_ref[...] = jnp.sum(total, axis=0, keepdims=True)


    blocks, pieces, spot = [], [], 0
    for act_ref, z_list, g_list, keep_ref in zip(acts, zs, gs, keeps):
        at = 0
        for z_ref, g_ref in zip(z_list, g_list):
            size = g_ref.shape[0]
            block = min(ROW_BLOCK, size)
            for base in range(0, size, block):
                blocks.append((g_ref, slice(base, base + block), act_ref, keep_ref, slice(at + base, at + base + block), slice(spot + base, spot + base + block)))
            pieces.append((z_ref, g_ref, act_ref, slice(at, at + size), slice(spot, spot + size)))
            at += size
            spot += size

    def grad_of(g_ref, rows):
        return dot_nn(g_ref[rows, :], dec_ref[...].reshape(-1, features))

    sums = jnp.zeros((8, features), F32)
    coming = grad_of(*blocks[0][:2])
    for at, (_, _, act_ref, keep_ref, local, place) in enumerate(blocks):
        grad_act = coming
        if at + 1 < len(blocks):
            coming = grad_of(*blocks[at + 1][:2])
        act = act_ref[local, :].astype(F32)
        slope = jnp.where(act < 2.0**-10, act * (1.0 - 0.5 * act), 1.0 - jnp.exp(-act))
        pre = (grad_act + wide(keep_ref[local, :], features) * norm_ref[...]) * slope
        sums = sums + jnp.sum(pre.reshape(-1, 8, features), axis=0)
        pre_s[place, :] = pre.astype(BF16)
    bias_ref[...] = jnp.sum(sums, axis=0, keepdims=True)
    dec_part = dec_in[...] if carried else None
    for _, g_ref, act_ref, local, _ in pieces:
        term = dot_tn(g_ref[...], act_ref[local, :])
        dec_part = term if dec_part is None else dec_part + term
    enc_part = enc_in[...] if carried else None
    for z_ref, _, _, _, place in pieces:
        term = dot_tn(z_ref[...], pre_s[place, :])
        enc_part = term if enc_part is None else enc_part + term
    if not parted:
        outs[0][...] = enc_part
        outs[1][...] = dec_part
        return
    keep_out, send_out = outs
    me = slots[0]
    for matrix, value in enumerate((enc_part, dec_part)):
        rows = value.shape[0] // parted
        for owner in range(parted):
            away = owner ^ me
            half = away // 2
            piece = value[owner * rows : (owner + 1) * rows, :]

            @pl.when(away % 2 == 0)
            def _():
                keep_out[pl.ds(half, 1), matrix] = piece[None]

            @pl.when(away % 2 == 1)
            def _():
                send_out[pl.ds(half, 1), matrix] = piece[None]


def backward(groups, keep_wide, norm_scaled, weights, carried, first, wide_by, parted, me):
    blocks, _, rows, _ = weights.shape
    width = blocks * rows
    counts = [len(zs) for _, zs, _, _ in groups]
    tokens = sum(act.shape[0] for act, _, _, _ in groups)
    fb = BACKWARD_BLOCK
    start = first // fb
    whole = lambda j, *_: (0, 0)
    across = lambda j, *_: (0, j + start)
    local = lambda j, *_: (0, j)
    operands, specs = [], []
    for act, zs, gs, keep_at in groups:
        size = act.shape[0]
        operands.append(act)
        specs.append(pl.BlockSpec((size, fb), across))
        for piece in (*zs, *gs):
            operands.append(piece)
            specs.append(pl.BlockSpec(piece.shape, whole, pipeline_mode=pl.Buffered(1)))
        operands.append(keep_wide)
        specs.append(pl.BlockSpec((size, LANES), lambda j, *_, at=keep_at // size: (at, 0)))
    operands += [norm_scaled, weights]
    specs += [pl.BlockSpec((1, fb), across), pl.BlockSpec((blocks, None, rows, fb), lambda j, *_: (0, 1, 0, j + start))]
    if carried is not None:
        operands += list(carried)
        specs += [pl.BlockSpec((width, fb), across)] * 2
    if parted:
        shape = (parted // 2, 2, width // parted, wide_by)
        block = pl.BlockSpec((parted // 2, 2, width // parted, fb), lambda j, *_: (0, 0, 0, j))
        out_shape = [jax.ShapeDtypeStruct(shape, F32)] * 2
        out_specs = [block] * 2
    else:
        out_shape = [jax.ShapeDtypeStruct((width, wide_by), F32)] * 2
        out_specs = [pl.BlockSpec((width, fb), local)] * 2
    out_shape += [jax.ShapeDtypeStruct((1, wide_by), F32), jax.ShapeDtypeStruct((1, width), F32)]
    out_specs += [pl.BlockSpec((1, fb), local), pl.BlockSpec((1, width), whole)]
    return pl.pallas_call(
        functools.partial(backward_kernel, counts, carried is not None, parted),
        grid_spec=pltpu.PrefetchScalarGridSpec(
            num_scalar_prefetch=1 if parted else 0,
            grid=(wide_by // fb,),
            in_specs=specs,
            out_specs=out_specs,
            scratch_shapes=[pltpu.VMEM((tokens, fb), BF16)],
        ),
        out_shape=out_shape,
        compiler_params=kernel_params(BACKWARD_VMEM),
        cost_estimate=pl.CostEstimate(
            flops=6 * tokens * width * wide_by // COST_SHARE,
            bytes_accessed=(2 * tokens * wide_by + 16 * width * wide_by) // COST_SHARE,
            transcendentals=tokens * wide_by // COST_SHARE,
        ),
        name="backward",
    )(*([me] if parted else []), *operands)


def ring_order(count):
    return list(range(0, count, 2)) + list(range(1, count, 2))[::-1]


def ring_shift(block, direction):
    order = ring_order(lax.axis_size("feat"))
    count = len(order)
    route = [(order[i], order[(i + direction) % count]) for i in range(count)]
    return lax.ppermute(block, "feat", route)


def swapped(block, axis, bit):
    return lax.ppermute(block, axis, [(i, i ^ bit) for i in range(lax.axis_size(axis))])


def summed(block, axes):
    for axis in axes:
        bit = 1
        while bit < lax.axis_size(axis):
            block = block + swapped(block, axis, bit)
            bit *= 2
    return block


def adamw(weight, grad, first, second, decay):
    first = BETA_ONE * first + (1.0 - BETA_ONE) * grad
    second = BETA_TWO * second + (1.0 - BETA_TWO) * grad * grad
    hat_first = first / (1.0 - BETA_ONE**STEP)
    hat_second = second / (1.0 - BETA_TWO**STEP)
    weight = weight - LEARN * (hat_first / (jnp.sqrt(hat_second) + EPSILON) + decay * weight)
    return (weight, first, second)


def shards(
    resid,
    segments,
    keep,
    ln_gain,
    ln_bias,
    qkv_weight,
    qkv_bias,
    enc_weight,
    enc_bias,
    dec_weight,
    dec_bias,
    enc_weight_m,
    enc_weight_v,
    enc_bias_m,
    enc_bias_v,
    dec_weight_m,
    dec_weight_v,
    dec_bias_m,
    dec_bias_v,
):
    own_rows, width = resid.shape
    group = keep.shape[0]
    feat_size, dp_size = lax.axis_size("feat"), lax.axis_size("dp")
    half = feat_size // 2
    features = enc_weight.shape[1]
    feat_at, dp_at = lax.axis_index("feat"), lax.axis_index("dp")
    everywhere = ("dp", "feat")

    me = dp_at.reshape(1).astype(jnp.int32)

    offset = feat_at * own_rows
    row_ids = jnp.arange(group, dtype=jnp.int32)
    seg_all = segments.reshape(group) + row_ids // ROW_LEN * ROW_LEN
    own_seg = lax.dynamic_slice_in_dim(seg_all, offset, own_rows)
    tail_seg = lax.dynamic_slice_in_dim(seg_all, jnp.maximum(offset - CTX, 0), CTX)
    tail_seg = jnp.where(feat_at > 0, tail_seg, -1)
    key_seg = jnp.concatenate([tail_seg, own_seg])[None]
    seg_wide = jnp.broadcast_to(own_seg[:, None], (own_rows, LANES))
    both = packed(enc_weight, dec_weight.T)
    weights = lax.all_gather(both, "dp")
    tail = lax.ppermute(resid[own_rows - CTX :], "feat", [(i, i + 1) for i in range(feat_size - 1)])
    tail, key_seg, seg_wide, both = together(tail, key_seg, seg_wide, both)
    tokens_z = attend(resid, tail, seg_wide, key_seg, ln_gain, ln_bias, qkv_weight, qkv_bias)

    tokens_z, keep = together(tokens_z, keep)
    z_stages = [[tokens_z]]
    right, left = tokens_z, tokens_z
    rows = own_rows // 2
    for hop in range(1, half):
        right, left = ring_shift(right, 1), ring_shift(left, -1)
        if hop == 1:
            order = jnp.asarray(ring_order(feat_size), jnp.int32)
            place = jnp.where(feat_at % 2 == 0, feat_at // 2, feat_size - 1 - feat_at // 2)
            keep_mask = keep.astype(F32)
            hops = []
            for away in range(1, half):
                hops += [-away, away]
            hops += [0, half]
            owners = order[(place + jnp.asarray(hops, jnp.int32)) % feat_size]
            keep_ring = keep_mask.reshape(feat_size, own_rows)[owners].reshape(group)
            keep_wide = jnp.broadcast_to(keep_ring[:, None], (group, LANES))
            own_keep = keep_ring[group - 2 * own_rows : group - own_rows][:, None]
            keep_total = jnp.sum(keep_mask)
            right, left, keep_wide, own_keep, keep_total = together(right, left, keep_wide, own_keep, keep_total)
        elif hop < half - 1:
            right, left = together(right, left)
        z_stages.append([right, left])
    right, left, weights = together(right, left, weights)
    z_stages[half - 1] = [right, left]
    keep_at = [group - 2 * own_rows] + [2 * (hop - 1) * own_rows for hop in range(1, half)] + [group - own_rows]
    z_float = tokens_z.astype(F32)
    acts, recs, stats = [None] * (half + 1), [None] * (half + 1), [None] * (half + 1)
    bias_row = enc_bias[None]

    def encoded(hop):
        acts[hop], recs[hop], stats[hop] = encode(
            z_stages[hop], keep_wide, keep_at[hop], weights, bias_row, hop == half
        )

    z_stages.append([ring_shift(right[:rows], 1), ring_shift(left[rows:], -1)])
    encoded(half - 1)
    z_stages[half], recs[half - 1], acts[half - 1] = together(z_stages[half], recs[half - 1], acts[half - 1])
    encoded(half)

    recs[half], weights = together(recs[half], weights)
    right, left = recs[half]
    for step in range(1, half + 1):
        right, left = ring_shift(right, 1), ring_shift(left, -1)
        if step == 1:
            dec_float = weights[:, 1].astype(F32)
            row_norm = jnp.sqrt(jnp.sum(dec_float * dec_float, axis=(0, 1)))[None]
            right, left, row_norm, z_stages[half - 2] = together(right, left, row_norm, z_stages[half - 2])
        elif step < half:
            hop = half - step
            encoded(hop)
            right, left, recs[hop], acts[hop], z_stages[hop - 1] = together(
                right, left, recs[hop], acts[hop], z_stages[hop - 1]
            )
        else:
            encoded(0)
            act_sum, fire_sum, square_sum = (sum(parts) for parts in zip(*stats))
            totals = jnp.stack([keep_total, jnp.sum(square_sum)])
            totals = jnp.pad(totals, (0, fire_sum.shape[1] - 2))[None]
            fired, act_total, totals = summed(jnp.concatenate([fire_sum, act_sum, totals]), ("dp",))
            counted, squares = totals[0], totals[1]
            mean_square = squares / (counted * width) + 1e-06
            unit = 2.0 / (width * mean_square * counted)
            norm_scaled = LAMBDA / counted * row_norm
            loss_part = LAMBDA * jnp.sum(act_sum * row_norm)
            penalty = (LAMBDA / counted) * act_total / row_norm[0]
            right, left, recs[0], acts[0], unit, norm_scaled, loss_part, penalty, fired = together(
                right, left, recs[0], acts[0], unit, norm_scaled, loss_part, penalty, fired
            )
            break
        from_left, from_right = recs[half - step]
        right, left = right.astype(F32), left.astype(F32)
        if step == 1:
            right = jnp.concatenate([from_right[:rows] + right, from_right[rows:]])
            left = jnp.concatenate([from_left[:rows], from_left[rows:] + left])
        else:
            right, left = from_right + right, from_left + left
        right, left = right.astype(BF16), left.astype(BF16)
    residue = recs[0][0] + right.astype(F32) + left.astype(F32) + dec_bias - z_float
    grad_out = own_keep * residue * unit
    fit_part = jnp.sum(own_keep * residue * residue) / (width * mean_square)
    loss_part = fit_part + loss_part
    own_grad = grad_out.astype(BF16)
    own_grad, loss_part = together(own_grad, loss_part)

    bias_share = out_bias_share = 0.0
    carried = None
    grad_stages = [[own_grad]]
    right, left = own_grad, own_grad

    def group_of(plan):
        return [(acts[hop], z_stages[hop], grad_stages[hop], keep_at[hop]) for hop in plan]

    for hop in range(1, half + 1):
        if hop == half:
            right, left = right[:rows], left[rows:]
        right, left = ring_shift(right, 1), ring_shift(left, -1)
        if hop < half:
            *carried, bias_grad, out_bias_grad = backward(
                group_of([hop - 1]), keep_wide, norm_scaled, weights, carried, 0, features, 0, None
            )
            bias_share, out_bias_share = bias_share + bias_grad, out_bias_share + out_bias_grad
        right, left, carried, bias_share, out_bias_share = together(right, left, carried, bias_share, out_bias_share)
        grad_stages.append([right, left])

    wide_by = features // LAST_PARTS
    kept, sent, aways, owns, last_bias = [], [], [], [], []
    scaled = norm_scaled
    for turn in range(LAST_PARTS + 2):
        coming = []
        if turn >= 2:
            away = aways[turn - 2]
            coming.append([swapped(block, "dp", 2 * other + 2) for other, block in enumerate(away)])
        else:
            coming.append([])
        coming.append(swapped(sent[turn - 1], "dp", 1) if 1 <= turn <= LAST_PARTS else None)
        if turn < LAST_PARTS:
            keep_part, send_part, bias_grad, out_bias_grad = backward(
                group_of([half - 1, half]), keep_wide, scaled, weights, carried, turn * wide_by, wide_by, dp_size, me
            )
            kept.append(keep_part)
            sent.append(send_part)
            last_bias.append(bias_grad)
        if turn == LAST_PARTS:
            bias_share = jnp.concatenate(
                [bias_share + jnp.concatenate(last_bias, axis=1), out_bias_share + out_bias_grad], axis=1
            )
            bias_share = summed(bias_share, ("dp",))[0]
        coming, scaled, sent, kept, bias_share = together(coming, scaled, sent, kept, bias_share)
        arrived, paired = coming
        if turn >= 2:
            owns[turn - 2] = owns[turn - 2] + sum(block.astype(F32) for block in arrived)
        if paired is not None:
            total = kept[turn - 1] + paired
            owns.append(total[0])
            aways.append([total[other].astype(BF16) for other in range(1, dp_size // 2)])
    enc_bias_grad, dec_bias_grad = bias_share[:features], bias_share[features:]
    own_dec = dec_weight.astype(BF16).astype(F32)
    own_squares = 0.0
    enc_grads, dec_grads = [], []
    for part in range(LAST_PARTS):
        span = slice(part * wide_by, (part + 1) * wide_by)
        enc_grads.append(owns[part][0])
        dec_grads.append(owns[part][1].T + penalty[span, None] * own_dec[span])
        own_squares = own_squares + jnp.sum(enc_grads[part] ** 2) + jnp.sum(dec_grads[part] ** 2)
    enc_grad = jnp.concatenate(enc_grads, axis=1)
    dec_grad = jnp.concatenate(dec_grads, axis=0)

    first_dp = dp_at == 0
    first_both = first_dp & (feat_at == 0)
    own_squares = own_squares + jnp.where(first_dp, jnp.sum(enc_bias_grad * enc_bias_grad), 0.0)
    own_squares = own_squares + jnp.where(first_both, jnp.sum(dec_bias_grad * dec_bias_grad), 0.0)
    total_squares, loss_total = summed(jnp.stack([own_squares, loss_part]), everywhere)
    overall_derivative_length = jnp.sqrt(total_squares)
    factor = jnp.minimum(1.0, CLIP_NORM / (overall_derivative_length + 1e-06))
    dec_new, dec_m, dec_v = adamw(dec_weight, dec_grad * factor, dec_weight_m, dec_weight_v, DECAY)
    row_squares = summed(jnp.sum(dec_new * dec_new, axis=1), ("dp",))
    enc_new, enc_m, enc_v = adamw(enc_weight, enc_grad * factor, enc_weight_m, enc_weight_v, DECAY)
    bias_new, bias_m, bias_v = adamw(enc_bias, enc_bias_grad * factor, enc_bias_m, enc_bias_v, 0.0)
    out_new, out_m, out_v = adamw(dec_bias, dec_bias_grad * factor, dec_bias_m, dec_bias_v, 0.0)
    dec_new = dec_new * lax.rsqrt(row_squares + 1e-12)[:, None]
    return (
        jnp.stack([loss_total, counted]),
        overall_derivative_length,
        fired,
        enc_new,
        enc_m,
        enc_v,
        bias_new,
        bias_m,
        bias_v,
        dec_new,
        dec_m,
        dec_v,
        out_new,
        out_m,
        out_v,
    )


def solution(mesh):
    return jax.shard_map(
        shards,
        mesh=mesh,
        in_specs=(
            P(("dp", "feat"), None),
            P("dp", None),
            P("dp"),
            P(),
            P(),
            P(),
            P(),
            P("dp", "feat"),
            P("feat"),
            P("feat", "dp"),
            P(),
            P("dp", "feat"),
            P("dp", "feat"),
            P("feat"),
            P("feat"),
            P("feat", "dp"),
            P("feat", "dp"),
            P(),
            P(),
        ),
        out_specs=(
            P(),
            P(),
            P("feat"),
            P("dp", "feat"),
            P("dp", "feat"),
            P("dp", "feat"),
            P("feat"),
            P("feat"),
            P("feat"),
            P("feat", "dp"),
            P("feat", "dp"),
            P("feat", "dp"),
            P(),
            P(),
            P(),
        ),
        check_vma=False,
    )
```

```python
import functools
import math

import jax
import jax.numpy as jnp
from jax import lax
from jax.experimental import pallas as pl
from jax.experimental.pallas import tpu as pltpu
from jax.sharding import PartitionSpec as P

HEAD = 64
ROW_LEN = 1024
CTX = 128
STEP = 10

LAMBDA = 0.001
CLIP_NORM = 0.004
LEARN = 0.02
BETA_ONE = 0.9
BETA_TWO = 0.999
EPSILON = 1e-08
DECAY = 0.01

ENCODE_BLOCK = 768
BACKWARD_BLOCK = 512
ROW_BLOCK = 512
LANES = 128
VMEM_BYTES = 60 * 2**20
LAST_PARTS = 3
PACK_BLOCK = 1536
COST_SHARE = 4
BF16 = jnp.bfloat16
F32 = jnp.float32


def kernel_params():
    return pltpu.CompilerParams(vmem_limit_bytes=VMEM_BYTES)


def dot_nn(a, b):
    return jnp.dot(a, b, preferred_element_type=F32)


def dot_nt(a, b):
    return lax.dot_general(a, b, (((1,), (1,)), ((), ())), preferred_element_type=F32)


def dot_tn(a, b):
    return lax.dot_general(a, b, (((0,), (0,)), ((), ())), preferred_element_type=F32)


def together(*values):
    leaves, tree = jax.tree.flatten(values)
    return jax.tree.unflatten(tree, lax.optimization_barrier(tuple(leaves)))


def normed(block, gain, shift):
    values = block.astype(F32)
    centred = values - jnp.mean(values, axis=1, keepdims=True)
    variance = jnp.mean(centred * centred, axis=1, keepdims=True)
    return (centred * lax.rsqrt(variance + 1e-05) * gain + shift).astype(BF16)


def project_kernel(rows_ref, gain_ref, bias_ref, w_ref, wb_ref, out_ref, normed_s):
    width = rows_ref.shape[1]

    @pl.when(pl.program_id(0) == 0)
    def _():
        gain = gain_ref[...].astype(F32).reshape(1, width)
        shift = bias_ref[...].astype(F32).reshape(1, width)
        normed_s[...] = normed(rows_ref[...], gain, shift)

    out_ref[...] = (dot_nn(normed_s[...], w_ref[...]) + wb_ref[...].astype(F32)).astype(BF16)


def project(resid, ln_gain, ln_bias, qkv_weight, qkv_bias):
    rows, width = resid.shape
    whole = lambda j: (0, 0)
    across = lambda j: (0, j)
    return pl.pallas_call(
        project_kernel,
        grid=(3,),
        in_specs=[
            pl.BlockSpec((rows, width), whole),
            pl.BlockSpec((width,), lambda j: (0,)),
            pl.BlockSpec((width,), lambda j: (0,)),
            pl.BlockSpec((width, width), across),
            pl.BlockSpec((1, width), across),
        ],
        out_specs=pl.BlockSpec((rows, width), across),
        out_shape=jax.ShapeDtypeStruct((rows, 3 * width), BF16),
        scratch_shapes=[pltpu.VMEM((rows, width), BF16)],
        compiler_params=kernel_params(),
        cost_estimate=pl.CostEstimate(flops=6 * rows * width * width, bytes_accessed=6 * width * width, transcendentals=0),
        name="project",
    )(resid, ln_gain, ln_bias, qkv_weight, qkv_bias[None])


def attend_kernel(own_ref, tail_ref, seg_q_ref, seg_k_ref, gain_ref, bias_ref, w_ref, wb_ref, z_ref, w_s, kv_s, sem):
    rows, width = z_ref.shape
    load = pltpu.make_async_copy(w_ref.at[:, pl.ds(width, 2 * width)], w_s, sem)
    load.start()
    lane = lax.broadcasted_iota(jnp.int32, (CTX, 2 * HEAD), 1)
    first_head = lane < HEAD
    place_q = lax.broadcasted_iota(jnp.int32, (CTX, 2 * CTX), 0) + CTX
    place_k = lax.broadcasted_iota(jnp.int32, (CTX, 2 * CTX), 1)
    earlier = place_k <= place_q

    def pairs_of(block, columns):
        if block > 0:
            return own_ref[(block - 1) * CTX : (block + 1) * CTX, columns]
        return jnp.concatenate([kv_s[:, columns.start - width : columns.stop - width], own_ref[:CTX, columns]], axis=0)

    for block in (*range(1, rows // CTX), 0):
        if block == 0:
            load.wait()
            gain = gain_ref[...].astype(F32).reshape(1, width)
            shift = bias_ref[...].astype(F32).reshape(1, width)
            offsets = wb_ref[...].astype(F32).reshape(1, 3 * width)
            tail = normed(tail_ref[...], gain, shift)
            kv_s[...] = (dot_nn(tail, w_s[...]) + offsets[:, width:]).astype(BF16)
        base = block * CTX
        seg_q = seg_q_ref[base : base + CTX, :]
        allowed = (jnp.concatenate([seg_q, seg_q], axis=1) == seg_k_ref[:, base : base + 2 * CTX]) & earlier
        allowed = jnp.concatenate([allowed, allowed], axis=0)
        starts = range(0, width, 2 * HEAD)
        scores = []
        for start in starts:
            query = own_ref[base : base + CTX, start : start + 2 * HEAD]
            keys = pairs_of(block, slice(width + start, width + start + 2 * HEAD))
            none = jnp.zeros_like(query)
            query = query * jnp.asarray(1.0 / math.sqrt(HEAD), BF16)
            query = jnp.concatenate([jnp.where(first_head, query, none), jnp.where(first_head, none, query)], axis=0)
            scores.append(dot_nt(query, keys))
        probs = []
        for part in scores:
            part = jnp.where(allowed, part, -1e30)
            expo = jnp.exp(part - jnp.max(part, axis=1, keepdims=True))
            probs.append((expo * (1.0 / jnp.sum(expo, axis=1, keepdims=True))).astype(BF16))
        for start, part in zip(starts, probs):
            values = pairs_of(block, slice(2 * width + start, 2 * width + start + 2 * HEAD))
            mixed = dot_nn(part, values)
            z_ref[base : base + CTX, start : start + 2 * HEAD] = jnp.where(first_head, mixed[:CTX], mixed[CTX:]).astype(BF16)


def attend(projected, tail, seg_q, seg_k, ln_gain, ln_bias, qkv_weight, qkv_bias):
    rows = projected.shape[0]
    width = tail.shape[1]
    vmem = pl.BlockSpec(memory_space=pltpu.VMEM)
    return pl.pallas_call(
        attend_kernel,
        in_specs=[vmem] * 6 + [pl.BlockSpec(memory_space=pl.ANY), vmem],
        out_specs=vmem,
        out_shape=jax.ShapeDtypeStruct((rows, width), BF16),
        scratch_shapes=[
            pltpu.VMEM((width, 2 * width), BF16),
            pltpu.VMEM((CTX, 2 * width), BF16),
            pltpu.SemaphoreType.DMA,
        ],
        compiler_params=kernel_params(),
        cost_estimate=pl.CostEstimate(
            flops=4 * rows * width * width, bytes_accessed=8 * width * width, transcendentals=rows * 2 * CTX * 12
        ),
        name="attend",
    )(projected, tail, seg_q, seg_k, ln_gain, ln_bias, qkv_weight, qkv_bias)


def packed_kernel(enc_ref, dec_ref, out_ref):
    out_ref[0] = enc_ref[...].astype(BF16)
    out_ref[1] = dec_ref[...].astype(BF16)


def packed(enc, dec):
    rows, columns = enc.shape
    block = PACK_BLOCK
    across = lambda j: (0, j)
    return pl.pallas_call(
        packed_kernel,
        grid=(columns // block,),
        in_specs=[pl.BlockSpec((rows, block), across)] * 2,
        out_specs=pl.BlockSpec((2, rows, block), lambda j: (0, 0, j)),
        out_shape=jax.ShapeDtypeStruct((2, rows, columns), BF16),
        compiler_params=kernel_params(),
        cost_estimate=pl.CostEstimate(flops=0, bytes_accessed=12 * rows * columns, transcendentals=0),
        name="packed",
    )(enc, dec)


def encode_kernel(count, rounded, *refs):
    z_refs, (keep_ref, enc_ref, bias_ref, dec_ref), rest = refs[:count], refs[count : count + 4], refs[count + 4 :]
    act_ref, rec_refs, (sum_ref, fire_ref, square_ref) = rest[0], rest[1 : 1 + count], rest[1 + count : 4 + count]
    totals = rest[4 + count :] if rounded else rec_refs
    step, last = pl.program_id(0), pl.num_programs(0) - 1
    features = enc_ref.shape[-1]

    def whole(ref):
        return ref[...].reshape(-1, features)

    @pl.when(step == 0)
    def _():
        spot, squares = 0, 0.0
        for total, z_ref in zip(totals, z_refs):
            total[...] = jnp.zeros_like(total)
            size, width = z_ref.shape
            values = z_ref[...].astype(F32)
            kept = wide(keep_ref[spot : spot + size, :], width) * values * values
            squares = squares + jnp.sum(kept.reshape(-1, 8, width), axis=0)
            spot += size
        square_ref[...] = jnp.sum(squares, axis=0, keepdims=True)

    blocks, spot = [], 0
    for piece in range(count):
        size = z_refs[piece].shape[0]
        block = min(ROW_BLOCK, size)
        for base in range(0, size, block):
            blocks.append((piece, slice(base, base + block), slice(spot + base, spot + base + block)))
        spot += size

    def preact_of(piece, rows):
        return dot_nn(z_refs[piece][rows, :], whole(enc_ref)) + bias_ref[...]

    sums = jnp.zeros((8, features), F32)
    fires = jnp.zeros((8, features), F32)
    coming = preact_of(*blocks[0][:2])
    for at, (piece, rows, place) in enumerate(blocks):
        preact = coming
        if at + 1 < len(blocks):
            coming = preact_of(*blocks[at + 1][:2])
        tiny = jnp.exp(-jnp.abs(preact))
        log_part = jnp.where(tiny < 2.0**-10, tiny * (1.0 - 0.5 * tiny), jnp.log(1.0 + tiny))
        act = jnp.maximum(preact, 0.0) + log_part
        low = act.astype(BF16)
        act_ref[place, :] = low
        kept = wide(keep_ref[place, :], features) * act
        sums = sums + jnp.sum(kept.reshape(-1, 8, features), axis=0)
        fires = fires + jnp.sum(jnp.tanh(kept).reshape(-1, 8, features), axis=0)
        totals[piece][rows, :] += dot_nt(low, whole(dec_ref))
    sum_ref[...] = jnp.sum(sums, axis=0, keepdims=True)
    fire_ref[...] = jnp.sum(fires, axis=0, keepdims=True)

    if rounded:

        @pl.when(step == last)
        def _():
            for piece in range(count):
                rec_refs[piece][...] = totals[piece][...].astype(BF16)


def wide(block, columns):
    return jnp.concatenate([block] * (columns // block.shape[1]), axis=1)


def encode(pieces, keep_wide, keep_at, weights, bias, rounded):
    parts, _, rows, features = weights.shape
    width = parts * rows
    sizes = [p.shape[0] for p in pieces]
    tokens = sum(sizes)
    fb = ENCODE_BLOCK
    whole = lambda j: (0, 0)
    across = lambda j: (0, j)
    keep_block = keep_at // tokens
    outs = pl.pallas_call(
        functools.partial(encode_kernel, len(pieces), rounded),
        grid=(features // fb,),
        in_specs=[pl.BlockSpec((s, width), whole) for s in sizes]
        + [
            pl.BlockSpec((tokens, LANES), lambda j: (keep_block, 0)),
            pl.BlockSpec((parts, None, rows, fb), lambda j: (0, 0, 0, j)),
            pl.BlockSpec((1, fb), across),
            pl.BlockSpec((parts, None, rows, fb), lambda j: (0, 1, 0, j)),
        ],
        out_specs=[pl.BlockSpec((tokens, fb), across)]
        + [pl.BlockSpec((s, width), whole) for s in sizes]
        + [pl.BlockSpec((1, fb), across)] * 2
        + [pl.BlockSpec((1, width), whole)],
        out_shape=[jax.ShapeDtypeStruct((tokens, features), BF16)]
        + [jax.ShapeDtypeStruct((s, width), BF16 if rounded else F32) for s in sizes]
        + [jax.ShapeDtypeStruct((1, features), F32)] * 2
        + [jax.ShapeDtypeStruct((1, width), F32)],
        scratch_shapes=[pltpu.VMEM((s, width), F32) for s in sizes] if rounded else [],
        compiler_params=kernel_params(),
        cost_estimate=pl.CostEstimate(
            flops=4 * tokens * width * features // COST_SHARE,
            bytes_accessed=2 * (2 * width * features + tokens * (features + 4 * width)) // COST_SHARE,
            transcendentals=3 * tokens * features // COST_SHARE,
        ),
        name="encode",
    )(*pieces, keep_wide, weights, bias, weights)
    return outs[0], outs[1 : 1 + len(pieces)], outs[-3:]


def joined_kernel(right_ref, left_ref, from_right_ref, from_left_ref, right_out, left_out):
    rows = right_ref.shape[0]
    right_out[:rows, :] = (from_right_ref[:rows, :] + right_ref[...].astype(F32)).astype(BF16)
    right_out[rows:, :] = from_right_ref[rows:, :].astype(BF16)
    left_out[:rows, :] = from_left_ref[:rows, :].astype(BF16)
    left_out[rows:, :] = (from_left_ref[rows:, :] + left_ref[...].astype(F32)).astype(BF16)


def joined(right, left, from_right, from_left):
    shape = jax.ShapeDtypeStruct(from_right.shape, BF16)
    return pl.pallas_call(
        joined_kernel, out_shape=[shape, shape], compiler_params=kernel_params(), name="joined"
    )(right, left, from_right, from_left)


def compared_kernel(rec_ref, right_ref, left_ref, z_ref, bias_ref, keep_ref, totals_ref, norm_ref, grad_ref, fit_ref, scaled_ref, penalty_ref, counted_ref):
    rows, width = z_ref.shape
    squares = jnp.sum(totals_ref[0:1, :], keepdims=True)
    counted = jnp.sum(totals_ref[1:2, :], keepdims=True)
    mean_square = squares / (counted * width) + 1e-06
    unit = 2.0 / (width * mean_square * counted)
    share = LAMBDA / counted
    norms = norm_ref[...]
    scaled_ref[...] = share * norms
    penalty_ref[...] = share / norms
    counted_ref[...] = counted + jnp.zeros(counted_ref.shape, F32)
    residue = rec_ref[...] + right_ref[...].astype(F32) + left_ref[...].astype(F32) + bias_ref[...] - z_ref[...].astype(F32)
    kept = wide(keep_ref[...], width) * residue
    grad_ref[...] = (kept * unit).astype(BF16)
    fit = jnp.sum((kept * residue).reshape(rows // 8, 8, width), axis=0)
    fit_ref[...] = sum(fit[:, at : at + LANES] for at in range(0, width, LANES)) / (width * mean_square)


def compared(rec, right, left, tokens_z, dec_bias, keep_wide, keep_at, totals, row_norm):
    rows, width = tokens_z.shape
    features = row_norm.shape[1]
    whole = lambda j: (0, 0)
    own = pl.BlockSpec((rows, width), whole)
    line = pl.BlockSpec((1, features), whole)
    tile = pl.BlockSpec((8, LANES), whole)
    return pl.pallas_call(
        compared_kernel,
        grid=(1,),
        in_specs=[own] * 4
        + [
            pl.BlockSpec((1, width), whole),
            pl.BlockSpec((rows, LANES), lambda j: (keep_at // rows, 0)),
            pl.BlockSpec(totals.shape, whole),
            line,
        ],
        out_specs=[own, tile, line, line, tile],
        out_shape=[
            jax.ShapeDtypeStruct((rows, width), BF16),
            jax.ShapeDtypeStruct((8, LANES), F32),
            jax.ShapeDtypeStruct((1, features), F32),
            jax.ShapeDtypeStruct((1, features), F32),
            jax.ShapeDtypeStruct((8, LANES), F32),
        ],
        compiler_params=kernel_params(),
        name="compared",
    )(rec, right, left, tokens_z, dec_bias, keep_wide, totals, row_norm)


def backward_kernel(groups, carried, parted, *refs):
    refs = list(refs)
    slots = refs.pop(0) if parted else None
    acts, zs, gs, keeps = [], [], [], []
    for count in groups:
        acts.append(refs.pop(0))
        zs.append([refs.pop(0) for _ in range(count)])
        gs.append([refs.pop(0) for _ in range(count)])
        keeps.append(refs.pop(0))
    norm_ref, dec_ref = refs.pop(0), refs.pop(0)
    enc_in, dec_in = (refs.pop(0), refs.pop(0)) if carried else (None, None)
    outs = [refs.pop(0) for _ in range(2)]
    bias_ref, out_bias_ref, pre_s = refs
    features = dec_ref.shape[-1]

    @pl.when(pl.program_id(0) == 0)
    def _():
        total = 0.0
        for g_list in gs:
            for g_ref in g_list:
                total = total + jnp.sum(g_ref[...].astype(F32).reshape(-1, 8, g_ref.shape[1]), axis=0)
        out_bias_ref[...] = jnp.sum(total, axis=0, keepdims=True)


    blocks, pieces, spot = [], [], 0
    for act_ref, z_list, g_list, keep_ref in zip(acts, zs, gs, keeps):
        at = 0
        for z_ref, g_ref in zip(z_list, g_list):
            size = g_ref.shape[0]
            block = min(ROW_BLOCK, size)
            for base in range(0, size, block):
                blocks.append((g_ref, slice(base, base + block), act_ref, keep_ref, slice(at + base, at + base + block), slice(spot + base, spot + base + block)))
            pieces.append((z_ref, g_ref, act_ref, slice(at, at + size), slice(spot, spot + size)))
            at += size
            spot += size

    def grad_of(g_ref, rows):
        return dot_nn(g_ref[rows, :], dec_ref[...].reshape(-1, features))

    sums = jnp.zeros((8, features), F32)
    coming = grad_of(*blocks[0][:2])
    for at, (_, _, act_ref, keep_ref, local, place) in enumerate(blocks):
        grad_act = coming
        if at + 1 < len(blocks):
            coming = grad_of(*blocks[at + 1][:2])
        act = act_ref[local, :].astype(F32)
        slope = jnp.where(act < 2.0**-10, act * (1.0 - 0.5 * act), 1.0 - jnp.exp(-act))
        pre = (grad_act + wide(keep_ref[local, :], features) * norm_ref[...]) * slope
        sums = sums + jnp.sum(pre.reshape(-1, 8, features), axis=0)
        pre_s[place, :] = pre.astype(BF16)
    bias_ref[...] = jnp.sum(sums, axis=0, keepdims=True)
    dec_part = dec_in[...] if carried else None
    for _, g_ref, act_ref, local, _ in pieces:
        term = dot_tn(g_ref[...], act_ref[local, :])
        dec_part = term if dec_part is None else dec_part + term
    enc_part = enc_in[...] if carried else None
    for z_ref, _, _, _, place in pieces:
        term = dot_tn(z_ref[...], pre_s[place, :])
        enc_part = term if enc_part is None else enc_part + term
    if not parted:
        outs[0][...] = enc_part
        outs[1][...] = dec_part
        return
    keep_out, send_out = outs
    me = slots[0]
    for matrix, value in enumerate((enc_part, dec_part)):
        rows = value.shape[0] // parted
        for owner in range(parted):
            away = owner ^ me
            half = away // 2
            piece = value[owner * rows : (owner + 1) * rows, :]

            @pl.when(away % 2 == 0)
            def _():
                keep_out[pl.ds(half, 1), matrix] = piece[None]

            @pl.when(away % 2 == 1)
            def _():
                send_out[pl.ds(half, 1), matrix] = piece[None].astype(send_out.dtype)


def backward(groups, keep_wide, norm_scaled, weights, carried, first, wide_by, parted, me):
    blocks, _, rows, _ = weights.shape
    width = blocks * rows
    counts = [len(zs) for _, zs, _, _ in groups]
    tokens = sum(act.shape[0] for act, _, _, _ in groups)
    fb = BACKWARD_BLOCK
    start = first // fb
    whole = lambda j, *_: (0, 0)
    across = lambda j, *_: (0, j + start)
    local = lambda j, *_: (0, j)
    operands, specs = [], []
    for act, zs, gs, keep_at in groups:
        size = act.shape[0]
        operands.append(act)
        specs.append(pl.BlockSpec((size, fb), across))
        for piece in (*zs, *gs):
            operands.append(piece)
            specs.append(pl.BlockSpec(piece.shape, whole, pipeline_mode=pl.Buffered(1)))
        operands.append(keep_wide)
        specs.append(pl.BlockSpec((size, LANES), lambda j, *_, at=keep_at // size: (at, 0)))
    operands += [norm_scaled, weights]
    specs += [pl.BlockSpec((1, fb), across), pl.BlockSpec((blocks, None, rows, fb), lambda j, *_: (0, 1, 0, j + start))]
    if carried is not None:
        operands += list(carried)
        specs += [pl.BlockSpec((width, fb), across)] * 2
    if parted:
        shape = (parted // 2, 2, width // parted, wide_by)
        block = pl.BlockSpec((parted // 2, 2, width // parted, fb), lambda j, *_: (0, 0, 0, j))
        out_shape = [jax.ShapeDtypeStruct(shape, F32), jax.ShapeDtypeStruct(shape, BF16)]
        out_specs = [block] * 2
    else:
        out_shape = [jax.ShapeDtypeStruct((width, wide_by), F32)] * 2
        out_specs = [pl.BlockSpec((width, fb), local)] * 2
    out_shape += [jax.ShapeDtypeStruct((1, wide_by), F32), jax.ShapeDtypeStruct((1, width), F32)]
    out_specs += [pl.BlockSpec((1, fb), local), pl.BlockSpec((1, width), whole)]
    return pl.pallas_call(
        functools.partial(backward_kernel, counts, carried is not None, parted),
        grid_spec=pltpu.PrefetchScalarGridSpec(
            num_scalar_prefetch=1 if parted else 0,
            grid=(wide_by // fb,),
            in_specs=specs,
            out_specs=out_specs,
            scratch_shapes=[pltpu.VMEM((tokens, fb), BF16)],
        ),
        out_shape=out_shape,
        compiler_params=kernel_params(),
        cost_estimate=pl.CostEstimate(
            flops=6 * tokens * width * wide_by // COST_SHARE,
            bytes_accessed=(2 * tokens * wide_by + 16 * width * wide_by) // COST_SHARE,
            transcendentals=tokens * wide_by // COST_SHARE,
        ),
        name="backward",
    )(*([me] if parted else []), *operands)


def finished_kernel(arrived_count, first, kept_ref, paired_ref, *refs):
    arrived, (penalty_ref, low_ref), rest = refs[:arrived_count], refs[arrived_count : arrived_count + 2], refs[arrived_count + 2 :]
    enc_ref, dec_ref, norm_ref = rest if first else rest[2:]
    grad = kept_ref[...] + paired_ref[...].astype(F32)
    for block in arrived:
        grad = grad + block[...].astype(F32)
    enc, dec = grad[0], grad[1] + penalty_ref[...] * low_ref[...].astype(F32)
    enc_ref[...] = enc
    dec_ref[...] = dec
    squares = enc * enc + dec * dec
    total = jnp.sum(squares.reshape(-1, 8, squares.shape[1]), axis=0)
    lanes = sum(total[:, at : at + LANES] for at in range(0, total.shape[1], LANES))

    @pl.when(pl.program_id(0) == 0)
    def _():
        norm_ref[...] = jnp.zeros_like(norm_ref)

    norm_ref[:8, :] += lanes


def finished(kept, paired, arrived, penalty, both, grads, part):
    _, _, rows, wide_by = kept.shape
    features = both.shape[2]
    fb = BACKWARD_BLOCK
    start = part * wide_by // fb
    own = pl.BlockSpec((None, 2, rows, fb), lambda j: (0, 0, 0, j))
    along = pl.BlockSpec((2, rows, fb), lambda j: (0, 0, j))
    first = grads is None
    return pl.pallas_call(
        functools.partial(finished_kernel, len(arrived), first),
        grid=(wide_by // fb,),
        in_specs=[own, own]
        + [along] * len(arrived)
        + [
            pl.BlockSpec((1, fb), lambda j: (0, j + start)),
            pl.BlockSpec((None, rows, fb), lambda j: (1, 0, j + start)),
        ]
        + ([] if first else [pl.BlockSpec(memory_space=pl.ANY)] * 2),
        out_specs=[pl.BlockSpec((rows, fb), lambda j: (0, j + start))] * 2 + [pl.BlockSpec((16, LANES), lambda j: (0, 0))],
        out_shape=[jax.ShapeDtypeStruct((rows, features), F32)] * 2 + [jax.ShapeDtypeStruct((16, LANES), F32)],
        input_output_aliases={} if first else {4 + len(arrived): 0, 5 + len(arrived): 1},
        compiler_params=kernel_params(),
        cost_estimate=pl.CostEstimate(flops=0, bytes_accessed=24 * rows * wide_by, transcendentals=0),
        name="finished",
    )(kept, paired, *arrived, penalty, both, *([] if first else grads))


def ring_order(count):
    return list(range(0, count, 2)) + list(range(1, count, 2))[::-1]


def ring_shift(block, direction):
    order = ring_order(lax.axis_size("feat"))
    count = len(order)
    route = [(order[i], order[(i + direction) % count]) for i in range(count)]
    return lax.ppermute(block, "feat", route)


def swapped(block, axis, bit):
    return lax.ppermute(block, axis, [(i, i ^ bit) for i in range(lax.axis_size(axis))])


def summed(block, axes):
    for axis in axes:
        size, bit = lax.axis_size(axis), 1
        while bit < size:
            if axis == "feat" and 4 * bit == size:
                first, second, third = (swapped(block, axis, bit * i) for i in (1, 2, 3))
                block = (block + first) + (second + third)
                bit *= 2
            else:
                block = block + swapped(block, axis, bit)
            bit *= 2
    return block


def adamw(weight, grad, first, second, decay):
    first = BETA_ONE * first + (1.0 - BETA_ONE) * grad
    second = BETA_TWO * second + (1.0 - BETA_TWO) * grad * grad
    hat_first = first / (1.0 - BETA_ONE**STEP)
    hat_second = second / (1.0 - BETA_TWO**STEP)
    weight = weight - LEARN * (hat_first / (jnp.sqrt(hat_second) + EPSILON) + decay * weight)
    return (weight, first, second)


def shards(
    resid,
    segments,
    keep,
    ln_gain,
    ln_bias,
    qkv_weight,
    qkv_bias,
    enc_weight,
    enc_bias,
    dec_weight,
    dec_bias,
    enc_weight_m,
    enc_weight_v,
    enc_bias_m,
    enc_bias_v,
    dec_weight_m,
    dec_weight_v,
    dec_bias_m,
    dec_bias_v,
):
    own_rows, width = resid.shape
    group = keep.shape[0]
    feat_size, dp_size = lax.axis_size("feat"), lax.axis_size("dp")
    half = feat_size // 2
    features = enc_weight.shape[1]
    feat_at, dp_at = lax.axis_index("feat"), lax.axis_index("dp")
    everywhere = ("dp", "feat")

    me = dp_at.reshape(1).astype(jnp.int32)

    offset = feat_at * own_rows
    row_ids = jnp.arange(group, dtype=jnp.int32)
    seg_all = segments.reshape(group) + row_ids // ROW_LEN * ROW_LEN
    own_seg = lax.dynamic_slice_in_dim(seg_all, offset, own_rows)
    tail_seg = lax.dynamic_slice_in_dim(seg_all, jnp.maximum(offset - CTX, 0), CTX)
    tail_seg = jnp.where(feat_at > 0, tail_seg, -1)
    key_seg = jnp.concatenate([tail_seg, own_seg])[None]
    seg_wide = jnp.broadcast_to(own_seg[:, None], (own_rows, LANES))
    both = packed(enc_weight, dec_weight.T)
    weights = lax.all_gather(both, "dp")
    tail = lax.ppermute(resid[own_rows - CTX :], "feat", [(i, (i + 1) % feat_size) for i in range(feat_size)])
    projected = project(resid, ln_gain, ln_bias, qkv_weight, qkv_bias)
    tail, key_seg, seg_wide, both, projected = together(tail, key_seg, seg_wide, both, projected)
    tokens_z = attend(projected, tail, seg_wide, key_seg, ln_gain, ln_bias, qkv_weight, qkv_bias)
    tokens_z, keep = together(tokens_z, keep)

    z_stages = [[tokens_z]]
    right, left = tokens_z, tokens_z
    rows = own_rows // 2
    for hop in range(1, half):
        right, left = ring_shift(right, 1), ring_shift(left, -1)
        if hop == 1:
            order = jnp.asarray(ring_order(feat_size), jnp.int32)
            place = jnp.where(feat_at % 2 == 0, feat_at // 2, feat_size - 1 - feat_at // 2)
            keep_mask = keep.astype(F32)
            hops = []
            for away in range(1, half):
                hops += [-away, away]
            hops += [0, half]
            owners = order[(place + jnp.asarray(hops, jnp.int32)) % feat_size]
            keep_ring = keep_mask.reshape(feat_size, own_rows)[owners].reshape(group)
            keep_wide = jnp.broadcast_to(keep_ring[:, None], (group, LANES))
            keep_total = jnp.pad(jnp.sum(keep_mask.reshape(-1, LANES), axis=0), (0, width - LANES))[None]
            right, left, keep_wide, keep_total = together(right, left, keep_wide, keep_total)
        elif hop < half - 1:
            right, left = together(right, left)
        z_stages.append([right, left])
    dec_float = weights[:, 1].astype(F32)
    row_norm = jnp.sqrt(jnp.sum(dec_float * dec_float, axis=(0, 1)))[None]
    near_squares = 0.0
    for hop in range(half - 1):
        for at, piece in enumerate(z_stages[hop]):
            first = group - 2 * own_rows if hop == 0 else (2 * (hop - 1) + at) * own_rows
            kept = keep_wide[first : first + own_rows, :1] * piece.astype(F32) ** 2
            near_squares = near_squares + jnp.sum(kept, axis=0, keepdims=True)
    right, left, weights, row_norm, near_squares = together(right, left, weights, row_norm, near_squares)
    z_stages[half - 1] = [right, left]
    keep_at = [group - 2 * own_rows] + [2 * (hop - 1) * own_rows for hop in range(1, half)] + [group - own_rows]
    acts, recs, stats = [None] * (half + 1), [None] * (half + 1), [None] * (half + 1)
    bias_row = enc_bias[None]

    def encoded(hop, pieces=slice(None)):
        chosen = z_stages[hop][pieces]
        at = keep_at[hop] + (own_rows if pieces == slice(1, 2) else 0)
        act, rec, stat = encode(chosen, keep_wide, at, weights, bias_row, hop == half)
        if pieces == slice(1, 2):
            act, rec, stat = [*acts[hop], act], [*recs[hop], *rec], [a + b for a, b in zip(stats[hop], stat)]
        elif pieces == slice(0, 1):
            act = [act]
        acts[hop], recs[hop], stats[hop] = act, list(rec), stat

    z_stages.append([ring_shift(right[:rows], 1), ring_shift(left[rows:], -1)])
    encoded(half - 1, slice(0, 1))
    z_stages[half], recs[half - 1], acts[half - 1] = together(z_stages[half], recs[half - 1], acts[half - 1])
    encoded(half)

    recs[half], weights, z_stages[half - 1] = together(recs[half], weights, z_stages[half - 1])
    right, left = recs[half]
    for step in range(1, half + 1):
        right, left = ring_shift(right, 1), ring_shift(left, -1)
        if step == 1:
            encoded(half - 1, slice(1, 2))
            far_squares = [stats[half - 1][2], stats[half][2]]
            right, left, recs[half - 1], acts[half - 1], far_squares = together(
                right, left, recs[half - 1], acts[half - 1], far_squares
            )
        elif step < half:
            hop = half - step
            encoded(hop)
            if step == 2:
                totals = jnp.concatenate([near_squares + far_squares[0] + far_squares[1], keep_total])
                totals = summed(totals, ("dp",))
            right, left, recs[hop], acts[hop], totals = together(right, left, recs[hop], acts[hop], totals)
        else:
            encoded(0)
            right, left, recs[0], acts[0], stats = together(right, left, recs[0], acts[0], stats)
            break
        from_left, from_right = recs[half - step]
        if step == 1:
            right, left = joined(right, left, from_right, from_left)
        else:
            right = (from_right + right.astype(F32)).astype(BF16)
            left = (from_left + left.astype(F32)).astype(BF16)
        following = half - step - 1
        right, left, z_stages[following] = together(right, left, z_stages[following])
    own_grad, fit_part, norm_scaled, penalty_scale, counted = compared(
        recs[0][0], right, left, tokens_z, dec_bias[None], keep_wide, keep_at[0], totals, row_norm
    )
    own_grad, fit_part, norm_scaled = together(own_grad, fit_part, norm_scaled)

    bias_shares, out_bias_shares = [], []
    carried = None
    grad_stages = [[own_grad]]
    right, left = own_grad, own_grad

    def group_of(plan):
        groups = []
        for hop in plan:
            zs, gs, at = z_stages[hop], grad_stages[hop], keep_at[hop]
            if isinstance(acts[hop], list):
                groups += [(act, [z], [g], at + i * own_rows) for i, (act, z, g) in enumerate(zip(acts[hop], zs, gs))]
            else:
                groups.append((acts[hop], zs, gs, at))
        return groups

    for hop in range(1, half + 1):
        if hop == half:
            right, left = right[:rows], left[rows:]
        right, left = ring_shift(right, 1), ring_shift(left, -1)
        if hop < half:
            *carried, bias_grad, out_bias_grad = backward(
                group_of([hop - 1]), keep_wide, norm_scaled, weights, carried, 0, features, 0, None
            )
            bias_shares.append(bias_grad)
            out_bias_shares.append(out_bias_grad)
        right, left, carried = together(right, left, carried)
        grad_stages.append([right, left])

    wide_by = features // LAST_PARTS
    kept, paired, arrived, last_bias = [], [], [], []
    grads = None

    def crossed(part):
        away = [kept[part][i] + paired[part][i].astype(F32) for i in range(1, dp_size // 2)]
        return [swapped(block.astype(BF16), "dp", 2 * i + 2) for i, block in enumerate(away)]

    def rest_of(block):
        for bit in range(2, dp_size, 2):
            if bit & (bit - 1) == 0:
                block = block + swapped(block, "dp", bit)
        return block

    act_sum, fire_sum, _ = (sum(parts) for parts in zip(*stats))
    counts = jnp.concatenate([fire_sum, act_sum])
    loss_share = LAMBDA * jnp.sum(act_sum * row_norm)
    sent = []
    for turn in range(LAST_PARTS):
        if turn >= 2:
            arrived.append(crossed(turn - 2))
        if turn == 2:
            counts = rest_of(counts)
        if turn >= 1:
            paired.append(swapped(sent[turn - 1], "dp", 1))
        if turn == 1:
            counts = counts + swapped(counts, "dp", 1)
        keep_part, send_part, bias_grad, out_bias_grad = backward(
            group_of([half - 1, half]), keep_wide, norm_scaled, weights, carried, turn * wide_by, wide_by, dp_size, me
        )
        kept.append(keep_part)
        sent.append(send_part)
        last_bias.append(bias_grad)
        arrived, paired, norm_scaled, sent, kept, last_bias, counts, loss_share = together(
            arrived, paired, norm_scaled, sent, kept, last_bias, counts, loss_share
        )
    fired, act_total = counts[0], counts[1:]
    penalty = penalty_scale * act_total
    arrived.append(crossed(LAST_PARTS - 2))
    paired.append(swapped(sent[-1], "dp", 1))
    arrived.append(crossed(LAST_PARTS - 1))
    bias_share = sum(bias_shares) + jnp.concatenate(last_bias, axis=1)
    out_bias_share = jnp.pad(sum(out_bias_shares) + out_bias_grad, ((0, 0), (0, features - width)))
    shares = jnp.concatenate([bias_share, out_bias_share])
    shares = rest_of(shares + swapped(shares, "dp", 1))
    enc_bias_grad, dec_bias_grad = shares[0], shares[1, :width]
    first_dp = dp_at == 0
    first_both = first_dp & (feat_at == 0)
    bias_squares = jnp.where(first_dp, jnp.sum(enc_bias_grad * enc_bias_grad), 0.0)
    bias_squares = bias_squares + jnp.where(first_both, jnp.sum(dec_bias_grad * dec_bias_grad), 0.0)
    row = lax.broadcasted_iota(jnp.int32, (16, LANES), 0)
    column = lax.broadcasted_iota(jnp.int32, (16, LANES), 1)
    norms = jnp.where((row == 0) & (column == 0), bias_squares, 0.0)
    norms = norms + jnp.where((row == 8) & (column == 0), loss_share, 0.0)
    norms = norms + jnp.pad(fit_part, ((8, 0), (0, 0)))
    for part in range(LAST_PARTS):
        *grads, part_norms = finished(kept[part], paired[part], arrived[part], penalty, both, grads, part)
        norms = norms + part_norms

    norms = summed(norms, everywhere)
    loss_total = jnp.sum(norms[8:])
    overall_derivative_length = jnp.sqrt(jnp.sum(norms[:8]))
    factor = jnp.minimum(1.0, CLIP_NORM / (overall_derivative_length + 1e-06))
    dec_new, dec_m, dec_v = adamw(dec_weight.T, grads[1] * factor, dec_weight_m.T, dec_weight_v.T, DECAY)
    row_squares = jnp.sum(dec_new * dec_new, axis=0, keepdims=True)
    row_squares = summed(row_squares, ("dp",))
    enc_new, enc_m, enc_v = adamw(enc_weight, grads[0] * factor, enc_weight_m, enc_weight_v, DECAY)
    bias_new, bias_m, bias_v = adamw(enc_bias, enc_bias_grad * factor, enc_bias_m, enc_bias_v, 0.0)
    out_new, out_m, out_v = adamw(dec_bias, dec_bias_grad * factor, dec_bias_m, dec_bias_v, 0.0)
    dec_new = (dec_new * lax.rsqrt(row_squares + 1e-12)).T
    dec_m, dec_v = dec_m.T, dec_v.T
    return (
        jnp.stack([loss_total, counted[0, 0]]),
        overall_derivative_length,
        fired,
        enc_new,
        enc_m,
        enc_v,
        bias_new,
        bias_m,
        bias_v,
        dec_new,
        dec_m,
        dec_v,
        out_new,
        out_m,
        out_v,
    )


def solution(mesh):
    return jax.shard_map(
        shards,
        mesh=mesh,
        in_specs=(
            P(("dp", "feat"), None),
            P("dp", None),
            P("dp"),
            P(),
            P(),
            P(),
            P(),
            P("dp", "feat"),
            P("feat"),
            P("feat", "dp"),
            P(),
            P("dp", "feat"),
            P("dp", "feat"),
            P("feat"),
            P("feat"),
            P("feat", "dp"),
            P("feat", "dp"),
            P(),
            P(),
        ),
        out_specs=(
            P(),
            P(),
            P("feat"),
            P("dp", "feat"),
            P("dp", "feat"),
            P("dp", "feat"),
            P("feat"),
            P("feat"),
            P("feat"),
            P("feat", "dp"),
            P("feat", "dp"),
            P("feat", "dp"),
            P(),
            P(),
            P(),
        ),
        check_vma=False,
    )
```

```python
import functools
import math

import jax
import jax.numpy as jnp
from jax import lax
from jax.experimental import pallas as pl
from jax.experimental.pallas import tpu as pltpu
from jax.sharding import PartitionSpec as P

HEAD = 64
ROW_LEN = 1024
CTX = 128
STEP = 10

LAMBDA = 0.001
CLIP_NORM = 0.004
LEARN = 0.02
BETA_ONE = 0.9
BETA_TWO = 0.999
EPSILON = 1e-08
DECAY = 0.01

ENCODE_BLOCK = 768
BACKWARD_BLOCK = 512
ROW_BLOCK = 512
LANES = 128
VMEM_BYTES = 60 * 2**20
LAST_PARTS = 3
PACK_BLOCK = 1536
COST_SHARE = 4
BF16 = jnp.bfloat16
F32 = jnp.float32


def kernel_params():
    return pltpu.CompilerParams(vmem_limit_bytes=VMEM_BYTES)


def dot_nn(a, b):
    return jnp.dot(a, b, preferred_element_type=F32)


def dot_nt(a, b):
    return lax.dot_general(a, b, (((1,), (1,)), ((), ())), preferred_element_type=F32)


def dot_tn(a, b):
    return lax.dot_general(a, b, (((0,), (0,)), ((), ())), preferred_element_type=F32)


def together(*values):
    leaves, tree = jax.tree.flatten(values)
    return jax.tree.unflatten(tree, lax.optimization_barrier(tuple(leaves)))


def normed(block, gain, shift):
    values = block.astype(F32)
    centred = values - jnp.mean(values, axis=1, keepdims=True)
    variance = jnp.mean(centred * centred, axis=1, keepdims=True)
    return (centred * lax.rsqrt(variance + 1e-05) * gain + shift).astype(BF16)


def project_kernel(rows_ref, gain_ref, bias_ref, w_ref, wb_ref, out_ref, normed_s, offset_s):
    width = rows_ref.shape[1]

    @pl.when(pl.program_id(0) == 0)
    def _():
        gain = gain_ref[...].astype(F32).reshape(1, width)
        shift = bias_ref[...].astype(F32).reshape(1, width)
        normed_s[...] = normed(rows_ref[...], gain, shift)
        offset_s[...] = wb_ref[...].astype(F32).reshape(1, 3 * width)

    at = pl.multiple_of(pl.program_id(0) * width, LANES)
    out_ref[...] = (dot_nn(normed_s[...], w_ref[...]) + offset_s[:, pl.ds(at, width)]).astype(BF16)


def project(resid, ln_gain, ln_bias, qkv_weight, qkv_bias):
    rows, width = resid.shape
    whole = lambda j: (0, 0)
    across = lambda j: (0, j)
    return pl.pallas_call(
        project_kernel,
        grid=(3,),
        in_specs=[
            pl.BlockSpec((rows, width), whole),
            pl.BlockSpec((width,), lambda j: (0,)),
            pl.BlockSpec((width,), lambda j: (0,)),
            pl.BlockSpec((width, width), across),
            pl.BlockSpec((3 * width,), lambda j: (0,)),
        ],
        out_specs=pl.BlockSpec((rows, width), across),
        out_shape=jax.ShapeDtypeStruct((rows, 3 * width), BF16),
        scratch_shapes=[pltpu.VMEM((rows, width), BF16), pltpu.VMEM((1, 3 * width), F32)],
        compiler_params=kernel_params(),
        cost_estimate=pl.CostEstimate(flops=6 * rows * width * width, bytes_accessed=6 * width * width, transcendentals=0),
        name="project",
    )(resid, ln_gain, ln_bias, qkv_weight, qkv_bias)


def attend_kernel(own_ref, tail_ref, seg_q_ref, seg_k_ref, gain_ref, bias_ref, w_ref, wb_ref, z_ref, w_s, kv_s, sem):
    rows, width = z_ref.shape
    load = pltpu.make_async_copy(w_ref.at[:, pl.ds(width, 2 * width)], w_s, sem)
    load.start()
    lane = lax.broadcasted_iota(jnp.int32, (CTX, 2 * HEAD), 1)
    first_head = lane < HEAD
    place_q = lax.broadcasted_iota(jnp.int32, (CTX, 2 * CTX), 0) + CTX
    place_k = lax.broadcasted_iota(jnp.int32, (CTX, 2 * CTX), 1)
    earlier = place_k <= place_q

    def pairs_of(block, columns):
        if block > 0:
            return own_ref[(block - 1) * CTX : (block + 1) * CTX, columns]
        return jnp.concatenate([kv_s[:, columns.start - width : columns.stop - width], own_ref[:CTX, columns]], axis=0)

    for block in (*range(1, rows // CTX), 0):
        if block == 0:
            load.wait()
            gain = gain_ref[...].astype(F32).reshape(1, width)
            shift = bias_ref[...].astype(F32).reshape(1, width)
            offsets = wb_ref[...].astype(F32).reshape(1, 3 * width)
            tail = normed(tail_ref[...], gain, shift)
            kv_s[...] = (dot_nn(tail, w_s[...]) + offsets[:, width:]).astype(BF16)
        base = block * CTX
        seg_q = seg_q_ref[base : base + CTX, :]
        allowed = (jnp.concatenate([seg_q, seg_q], axis=1) == seg_k_ref[:, base : base + 2 * CTX]) & earlier
        allowed = jnp.concatenate([allowed, allowed], axis=0)
        starts = range(0, width, 2 * HEAD)
        scores = []
        for start in starts:
            query = own_ref[base : base + CTX, start : start + 2 * HEAD]
            keys = pairs_of(block, slice(width + start, width + start + 2 * HEAD))
            none = jnp.zeros_like(query)
            query = query * jnp.asarray(1.0 / math.sqrt(HEAD), BF16)
            query = jnp.concatenate([jnp.where(first_head, query, none), jnp.where(first_head, none, query)], axis=0)
            scores.append(dot_nt(query, keys))
        probs = []
        for part in scores:
            part = jnp.where(allowed, part, -1e30)
            expo = jnp.exp(part - jnp.max(part, axis=1, keepdims=True))
            probs.append((expo * (1.0 / jnp.sum(expo, axis=1, keepdims=True))).astype(BF16))
        for start, part in zip(starts, probs):
            values = pairs_of(block, slice(2 * width + start, 2 * width + start + 2 * HEAD))
            mixed = dot_nn(part, values)
            z_ref[base : base + CTX, start : start + 2 * HEAD] = jnp.where(first_head, mixed[:CTX], mixed[CTX:]).astype(BF16)


def attend(projected, tail, seg_q, seg_k, ln_gain, ln_bias, qkv_weight, qkv_bias):
    rows = projected.shape[0]
    width = tail.shape[1]
    vmem = pl.BlockSpec(memory_space=pltpu.VMEM)
    return pl.pallas_call(
        attend_kernel,
        in_specs=[vmem] * 6 + [pl.BlockSpec(memory_space=pl.ANY), vmem],
        out_specs=vmem,
        out_shape=jax.ShapeDtypeStruct((rows, width), BF16),
        scratch_shapes=[
            pltpu.VMEM((width, 2 * width), BF16),
            pltpu.VMEM((CTX, 2 * width), BF16),
            pltpu.SemaphoreType.DMA,
        ],
        compiler_params=kernel_params(),
        cost_estimate=pl.CostEstimate(
            flops=4 * rows * width * width, bytes_accessed=8 * width * width, transcendentals=rows * 2 * CTX * 12
        ),
        name="attend",
    )(projected, tail, seg_q, seg_k, ln_gain, ln_bias, qkv_weight, qkv_bias)


def packed_kernel(enc_ref, dec_ref, out_ref):
    out_ref[0] = enc_ref[...].astype(BF16)
    out_ref[1] = dec_ref[...].astype(BF16)


def packed(enc, dec):
    rows, columns = enc.shape
    block = PACK_BLOCK
    across = lambda j: (0, j)
    return pl.pallas_call(
        packed_kernel,
        grid=(columns // block,),
        in_specs=[pl.BlockSpec((rows, block), across)] * 2,
        out_specs=pl.BlockSpec((2, rows, block), lambda j: (0, 0, j)),
        out_shape=jax.ShapeDtypeStruct((2, rows, columns), BF16),
        compiler_params=kernel_params(),
        cost_estimate=pl.CostEstimate(flops=0, bytes_accessed=12 * rows * columns, transcendentals=0),
        name="packed",
    )(enc, dec)


def encode_kernel(count, *refs):
    z_refs, (keep_ref, enc_ref, bias_ref, dec_ref), rest = refs[:count], refs[count : count + 4], refs[count + 4 :]
    act_ref, rec_refs, (sum_ref, fire_ref, square_ref) = rest[0], rest[1 : 1 + count], rest[1 + count : 4 + count]
    totals = rest[4 + count :]
    step, last = pl.program_id(0), pl.num_programs(0) - 1
    features = enc_ref.shape[-1]

    def whole(ref):
        return ref[...].reshape(-1, features)

    @pl.when(step == 0)
    def _():
        spot, squares = 0, 0.0
        for total, z_ref in zip(totals, z_refs):
            total[...] = jnp.zeros_like(total)
            size, width = z_ref.shape
            values = z_ref[...].astype(F32)
            kept = wide(keep_ref[spot : spot + size, :], width) * values * values
            squares = squares + jnp.sum(kept.reshape(-1, 8, width), axis=0)
            spot += size
        square_ref[...] = jnp.sum(squares, axis=0, keepdims=True)

    blocks, spot = [], 0
    for piece in range(count):
        size = z_refs[piece].shape[0]
        block = min(ROW_BLOCK, size)
        for base in range(0, size, block):
            blocks.append((piece, slice(base, base + block), slice(spot + base, spot + base + block)))
        spot += size

    def preact_of(piece, rows):
        return dot_nn(z_refs[piece][rows, :], whole(enc_ref)) + bias_ref[...]

    sums = jnp.zeros((8, features), F32)
    fires = jnp.zeros((8, features), F32)
    coming = preact_of(*blocks[0][:2])
    for at, (piece, rows, place) in enumerate(blocks):
        preact = coming
        if at + 1 < len(blocks):
            coming = preact_of(*blocks[at + 1][:2])
        tiny = jnp.exp(-jnp.abs(preact))
        log_part = jnp.where(tiny < 2.0**-10, tiny * (1.0 - 0.5 * tiny), jnp.log(1.0 + tiny))
        act = jnp.maximum(preact, 0.0) + log_part
        low = act.astype(BF16)
        act_ref[place, :] = low
        kept = wide(keep_ref[place, :], features) * act
        sums = sums + jnp.sum(kept.reshape(-1, 8, features), axis=0)
        fires = fires + jnp.sum(jnp.tanh(kept).reshape(-1, 8, features), axis=0)
        totals[piece][rows, :] += dot_nt(low, whole(dec_ref))
    sum_ref[...] = jnp.sum(sums, axis=0, keepdims=True)
    fire_ref[...] = jnp.sum(fires, axis=0, keepdims=True)

    @pl.when(step == last)
    def _():
        for piece in range(count):
            rec_refs[piece][...] = totals[piece][...].astype(BF16)


def wide(block, columns):
    return jnp.concatenate([block] * (columns // block.shape[1]), axis=1)


def encode(pieces, keep_wide, keep_at, weights, bias):
    parts, _, rows, features = weights.shape
    width = parts * rows
    sizes = [p.shape[0] for p in pieces]
    tokens = sum(sizes)
    fb = ENCODE_BLOCK
    whole = lambda j: (0, 0)
    across = lambda j: (0, j)
    keep_block = keep_at // tokens
    outs = pl.pallas_call(
        functools.partial(encode_kernel, len(pieces)),
        grid=(features // fb,),
        in_specs=[pl.BlockSpec((s, width), whole) for s in sizes]
        + [
            pl.BlockSpec((tokens, LANES), lambda j: (keep_block, 0)),
            pl.BlockSpec((parts, None, rows, fb), lambda j: (0, 0, 0, j)),
            pl.BlockSpec((1, fb), across),
            pl.BlockSpec((parts, None, rows, fb), lambda j: (0, 1, 0, j)),
        ],
        out_specs=[pl.BlockSpec((tokens, fb), across)]
        + [pl.BlockSpec((s, width), whole) for s in sizes]
        + [pl.BlockSpec((1, fb), across)] * 2
        + [pl.BlockSpec((1, width), whole)],
        out_shape=[jax.ShapeDtypeStruct((tokens, features), BF16)]
        + [jax.ShapeDtypeStruct((s, width), BF16) for s in sizes]
        + [jax.ShapeDtypeStruct((1, features), F32)] * 2
        + [jax.ShapeDtypeStruct((1, width), F32)],
        scratch_shapes=[pltpu.VMEM((s, width), F32) for s in sizes],
        compiler_params=kernel_params(),
        cost_estimate=pl.CostEstimate(
            flops=4 * tokens * width * features // COST_SHARE,
            bytes_accessed=2 * (2 * width * features + tokens * (features + 4 * width)) // COST_SHARE,
            transcendentals=3 * tokens * features // COST_SHARE,
        ),
        name="encode",
    )(*pieces, keep_wide, weights, bias, weights)
    return outs[0], outs[1 : 1 + len(pieces)], outs[-3:]


def joined_kernel(right_ref, left_ref, from_right_ref, from_left_ref, right_out, left_out):
    rows = right_ref.shape[0]
    right_out[:rows, :] = (from_right_ref[:rows, :].astype(F32) + right_ref[...].astype(F32)).astype(BF16)
    right_out[rows:, :] = from_right_ref[rows:, :]
    left_out[:rows, :] = from_left_ref[:rows, :]
    left_out[rows:, :] = (from_left_ref[rows:, :].astype(F32) + left_ref[...].astype(F32)).astype(BF16)


def joined(right, left, from_right, from_left):
    rows, width = from_right.shape
    half = pl.BlockSpec((rows // 2, 2 * LANES), lambda j: (0, j))
    full = pl.BlockSpec((rows, 2 * LANES), lambda j: (0, j))
    return pl.pallas_call(
        joined_kernel,
        grid=(width // (2 * LANES),),
        in_specs=[half, half, full, full],
        out_specs=[full, full],
        out_shape=[jax.ShapeDtypeStruct((rows, width), BF16)] * 2,
        compiler_params=kernel_params(),
        name="joined",
    )(right, left, from_right, from_left)


def compared_kernel(rec_ref, right_ref, left_ref, z_ref, bias_ref, keep_ref, totals_ref, norm_ref, grad_ref, fit_ref, scaled_ref, penalty_ref, counted_ref):
    rows, width = z_ref.shape
    squares = jnp.sum(totals_ref[0:1, :], keepdims=True)
    counted = jnp.sum(totals_ref[1:2, :], keepdims=True)
    mean_square = squares / (counted * width) + 1e-06
    unit = 2.0 / (width * mean_square * counted)
    residue = rec_ref[...].astype(F32) + right_ref[...].astype(F32) + left_ref[...].astype(F32)
    residue = residue + bias_ref[...] - z_ref[...].astype(F32)
    kept = wide(keep_ref[...], width) * residue
    grad_ref[...] = (kept * unit).astype(BF16)
    fit = jnp.sum((kept * residue).reshape(rows // 8, 8, width), axis=0)

    @pl.when(pl.program_id(0) == 0)
    def _():
        share = LAMBDA / counted
        norms = norm_ref[...]
        scaled_ref[...] = share * norms
        penalty_ref[...] = share / norms
        counted_ref[...] = counted + jnp.zeros(counted_ref.shape, F32)
        fit_ref[...] = jnp.zeros_like(fit_ref)

    fit_ref[...] += sum(fit[:, at : at + LANES] for at in range(0, width, LANES)) / (width * mean_square)


def compared(rec, right, left, tokens_z, dec_bias, keep_wide, keep_at, totals, row_norm):
    rows, width = tokens_z.shape
    features = row_norm.shape[1]
    block = CTX
    whole = lambda j: (0, 0)
    own = pl.BlockSpec((block, width), lambda j: (j, 0))
    line = pl.BlockSpec((1, features), whole)
    tile = pl.BlockSpec((8, LANES), whole)
    return pl.pallas_call(
        compared_kernel,
        grid=(rows // block,),
        in_specs=[own] * 4
        + [
            pl.BlockSpec((1, width), whole),
            pl.BlockSpec((block, LANES), lambda j: (keep_at // block + j, 0)),
            pl.BlockSpec(totals.shape, whole),
            line,
        ],
        out_specs=[own, tile, line, line, tile],
        out_shape=[
            jax.ShapeDtypeStruct((rows, width), BF16),
            jax.ShapeDtypeStruct((8, LANES), F32),
            jax.ShapeDtypeStruct((1, features), F32),
            jax.ShapeDtypeStruct((1, features), F32),
            jax.ShapeDtypeStruct((8, LANES), F32),
        ],
        compiler_params=kernel_params(),
        name="compared",
    )(rec, right, left, tokens_z, dec_bias, keep_wide, totals, row_norm)


def backward_kernel(groups, carried, parted, *refs):
    refs = list(refs)
    slots = refs.pop(0) if parted else None
    acts, zs, gs, keeps = [], [], [], []
    for count in groups:
        acts.append(refs.pop(0))
        zs.append([refs.pop(0) for _ in range(count)])
        gs.append([refs.pop(0) for _ in range(count)])
        keeps.append(refs.pop(0))
    norm_ref, dec_ref = refs.pop(0), refs.pop(0)
    enc_in, dec_in = (refs.pop(0), refs.pop(0)) if carried else (None, None)
    outs = [refs.pop(0) for _ in range(2)]
    bias_ref, out_bias_ref, pre_s = refs
    features = dec_ref.shape[-1]

    @pl.when(pl.program_id(0) == 0)
    def _():
        total = 0.0
        for g_list in gs:
            for g_ref in g_list:
                total = total + jnp.sum(g_ref[...].astype(F32).reshape(-1, 8, g_ref.shape[1]), axis=0)
        out_bias_ref[...] = jnp.sum(total, axis=0, keepdims=True)


    blocks, pieces, spot = [], [], 0
    for act_ref, z_list, g_list, keep_ref in zip(acts, zs, gs, keeps):
        at = 0
        for z_ref, g_ref in zip(z_list, g_list):
            size = g_ref.shape[0]
            block = min(ROW_BLOCK, size)
            for base in range(0, size, block):
                blocks.append((g_ref, slice(base, base + block), act_ref, keep_ref, slice(at + base, at + base + block), slice(spot + base, spot + base + block)))
            pieces.append((z_ref, g_ref, act_ref, slice(at, at + size), slice(spot, spot + size)))
            at += size
            spot += size

    def grad_of(g_ref, rows):
        return dot_nn(g_ref[rows, :], dec_ref[...].reshape(-1, features))

    sums = jnp.zeros((8, features), F32)
    coming = grad_of(*blocks[0][:2])
    for at, (_, _, act_ref, keep_ref, local, place) in enumerate(blocks):
        grad_act = coming
        if at + 1 < len(blocks):
            coming = grad_of(*blocks[at + 1][:2])
        act = act_ref[local, :].astype(F32)
        slope = jnp.where(act < 2.0**-10, act * (1.0 - 0.5 * act), 1.0 - jnp.exp(-act))
        pre = (grad_act + wide(keep_ref[local, :], features) * norm_ref[...]) * slope
        sums = sums + jnp.sum(pre.reshape(-1, 8, features), axis=0)
        pre_s[place, :] = pre.astype(BF16)
    bias_ref[...] = jnp.sum(sums, axis=0, keepdims=True)
    dec_part = dec_in[...] if carried else None
    for _, g_ref, act_ref, local, _ in pieces:
        term = dot_tn(g_ref[...], act_ref[local, :])
        dec_part = term if dec_part is None else dec_part + term
    enc_part = enc_in[...] if carried else None
    for z_ref, _, _, _, place in pieces:
        term = dot_tn(z_ref[...], pre_s[place, :])
        enc_part = term if enc_part is None else enc_part + term
    if not parted:
        outs[0][...] = enc_part
        outs[1][...] = dec_part
        return
    keep_out, send_out = outs
    me = slots[0]
    for matrix, value in enumerate((enc_part, dec_part)):
        rows = value.shape[0] // parted
        for owner in range(parted):
            away = owner ^ me
            half = away // 2
            piece = value[owner * rows : (owner + 1) * rows, :]

            @pl.when(away % 2 == 0)
            def _():
                keep_out[pl.ds(half, 1), matrix] = piece[None]

            @pl.when(away % 2 == 1)
            def _():
                send_out[pl.ds(half, 1), matrix] = piece[None].astype(send_out.dtype)


def backward(groups, keep_wide, norm_scaled, weights, carried, first, wide_by, parted, me):
    blocks, _, rows, _ = weights.shape
    width = blocks * rows
    counts = [len(zs) for _, zs, _, _ in groups]
    tokens = sum(act.shape[0] for act, _, _, _ in groups)
    fb = BACKWARD_BLOCK
    start = first // fb
    whole = lambda j, *_: (0, 0)
    across = lambda j, *_: (0, j + start)
    local = lambda j, *_: (0, j)
    operands, specs = [], []
    for act, zs, gs, keep_at in groups:
        size = act.shape[0]
        operands.append(act)
        specs.append(pl.BlockSpec((size, fb), across))
        for piece in (*zs, *gs):
            operands.append(piece)
            specs.append(pl.BlockSpec(piece.shape, whole, pipeline_mode=pl.Buffered(1)))
        operands.append(keep_wide)
        specs.append(pl.BlockSpec((size, LANES), lambda j, *_, at=keep_at // size: (at, 0)))
    operands += [norm_scaled, weights]
    specs += [pl.BlockSpec((1, fb), across), pl.BlockSpec((blocks, None, rows, fb), lambda j, *_: (0, 1, 0, j + start))]
    if carried is not None:
        operands += list(carried)
        specs += [pl.BlockSpec((width, fb), across)] * 2
    if parted:
        shape = (parted // 2, 2, width // parted, wide_by)
        block = pl.BlockSpec((parted // 2, 2, width // parted, fb), lambda j, *_: (0, 0, 0, j))
        out_shape = [jax.ShapeDtypeStruct(shape, F32), jax.ShapeDtypeStruct(shape, BF16)]
        out_specs = [block] * 2
    else:
        out_shape = [jax.ShapeDtypeStruct((width, wide_by), F32)] * 2
        out_specs = [pl.BlockSpec((width, fb), local)] * 2
    out_shape += [jax.ShapeDtypeStruct((1, wide_by), F32), jax.ShapeDtypeStruct((1, width), F32)]
    out_specs += [pl.BlockSpec((1, fb), local), pl.BlockSpec((1, width), whole)]
    return pl.pallas_call(
        functools.partial(backward_kernel, counts, carried is not None, parted),
        grid_spec=pltpu.PrefetchScalarGridSpec(
            num_scalar_prefetch=1 if parted else 0,
            grid=(wide_by // fb,),
            in_specs=specs,
            out_specs=out_specs,
            scratch_shapes=[pltpu.VMEM((tokens, fb), BF16)],
        ),
        out_shape=out_shape,
        compiler_params=kernel_params(),
        cost_estimate=pl.CostEstimate(
            flops=6 * tokens * width * wide_by // COST_SHARE,
            bytes_accessed=(2 * tokens * wide_by + 16 * width * wide_by) // COST_SHARE,
            transcendentals=tokens * wide_by // COST_SHARE,
        ),
        name="backward",
    )(*([me] if parted else []), *operands)


def finished_kernel(arrived_count, first, kept_ref, paired_ref, *refs):
    arrived, (penalty_ref, low_ref), rest = refs[:arrived_count], refs[arrived_count : arrived_count + 2], refs[arrived_count + 2 :]
    enc_ref, dec_ref, norm_ref = rest if first else rest[2:]
    grad = kept_ref[...] + paired_ref[...].astype(F32)
    for block in arrived:
        grad = grad + block[...].astype(F32)
    enc, dec = grad[0], grad[1] + penalty_ref[...] * low_ref[...].astype(F32)
    enc_ref[...] = enc
    dec_ref[...] = dec
    squares = enc * enc + dec * dec
    total = jnp.sum(squares.reshape(-1, 8, squares.shape[1]), axis=0)
    lanes = sum(total[:, at : at + LANES] for at in range(0, total.shape[1], LANES))

    @pl.when(pl.program_id(0) == 0)
    def _():
        norm_ref[...] = jnp.zeros_like(norm_ref)

    norm_ref[:8, :] += lanes


def finished(kept, paired, arrived, penalty, both, grads, part):
    _, _, rows, wide_by = kept.shape
    features = both.shape[2]
    fb = BACKWARD_BLOCK
    start = part * wide_by // fb
    own = pl.BlockSpec((None, 2, rows, fb), lambda j: (0, 0, 0, j))
    along = pl.BlockSpec((2, rows, fb), lambda j: (0, 0, j))
    first = grads is None
    return pl.pallas_call(
        functools.partial(finished_kernel, len(arrived), first),
        grid=(wide_by // fb,),
        in_specs=[own, own]
        + [along] * len(arrived)
        + [
            pl.BlockSpec((1, fb), lambda j: (0, j + start)),
            pl.BlockSpec((None, rows, fb), lambda j: (1, 0, j + start)),
        ]
        + ([] if first else [pl.BlockSpec(memory_space=pl.ANY)] * 2),
        out_specs=[pl.BlockSpec((rows, fb), lambda j: (0, j + start))] * 2 + [pl.BlockSpec((16, LANES), lambda j: (0, 0))],
        out_shape=[jax.ShapeDtypeStruct((rows, features), F32)] * 2 + [jax.ShapeDtypeStruct((16, LANES), F32)],
        input_output_aliases={} if first else {4 + len(arrived): 0, 5 + len(arrived): 1},
        compiler_params=kernel_params(),
        cost_estimate=pl.CostEstimate(flops=0, bytes_accessed=24 * rows * wide_by, transcendentals=0),
        name="finished",
    )(kept, paired, *arrived, penalty, both, *([] if first else grads))


def ring_order(count):
    return list(range(0, count, 2)) + list(range(1, count, 2))[::-1]


def ring_shift(block, direction):
    order = ring_order(lax.axis_size("feat"))
    count = len(order)
    route = [(order[i], order[(i + direction) % count]) for i in range(count)]
    return lax.ppermute(block, "feat", route)


def swapped(block, axis, bit):
    return lax.ppermute(block, axis, [(i, i ^ bit) for i in range(lax.axis_size(axis))])


def summed(block, axes):
    for axis in axes:
        size, bit = lax.axis_size(axis), 1
        while bit < size:
            block = block + swapped(block, axis, bit)
            bit *= 2
    return block


def adamw(weight, grad, first, second, decay):
    first = BETA_ONE * first + (1.0 - BETA_ONE) * grad
    second = BETA_TWO * second + (1.0 - BETA_TWO) * grad * grad
    hat_first = first / (1.0 - BETA_ONE**STEP)
    hat_second = second / (1.0 - BETA_TWO**STEP)
    weight = weight - LEARN * (hat_first / (jnp.sqrt(hat_second) + EPSILON) + decay * weight)
    return (weight, first, second)


def shards(
    resid,
    segments,
    keep,
    ln_gain,
    ln_bias,
    qkv_weight,
    qkv_bias,
    enc_weight,
    enc_bias,
    dec_weight,
    dec_bias,
    enc_weight_m,
    enc_weight_v,
    enc_bias_m,
    enc_bias_v,
    dec_weight_m,
    dec_weight_v,
    dec_bias_m,
    dec_bias_v,
):
    own_rows, width = resid.shape
    group = keep.shape[0]
    feat_size, dp_size = lax.axis_size("feat"), lax.axis_size("dp")
    half = feat_size // 2
    features = enc_weight.shape[1]
    feat_at, dp_at = lax.axis_index("feat"), lax.axis_index("dp")
    everywhere = ("dp", "feat")

    me = dp_at.reshape(1).astype(jnp.int32)

    offset = feat_at * own_rows
    row_ids = jnp.arange(group, dtype=jnp.int32)
    seg_all = segments.reshape(group) + row_ids // ROW_LEN * ROW_LEN
    own_seg = lax.dynamic_slice_in_dim(seg_all, offset, own_rows)
    tail_seg = lax.dynamic_slice_in_dim(seg_all, jnp.maximum(offset - CTX, 0), CTX)
    tail_seg = jnp.where(feat_at > 0, tail_seg, -1)
    key_seg = jnp.concatenate([tail_seg, own_seg])[None]
    seg_wide = jnp.broadcast_to(own_seg[:, None], (own_rows, LANES))
    both = packed(enc_weight, dec_weight.T)
    weights = lax.all_gather(both, "dp")
    tail = lax.ppermute(resid[own_rows - CTX :], "feat", [(i, (i + 1) % feat_size) for i in range(feat_size)])
    projected = project(resid, ln_gain, ln_bias, qkv_weight, qkv_bias)
    tail, key_seg, seg_wide, both, projected = together(tail, key_seg, seg_wide, both, projected)
    tokens_z = attend(projected, tail, seg_wide, key_seg, ln_gain, ln_bias, qkv_weight, qkv_bias)
    tokens_z, keep = together(tokens_z, keep)

    z_stages = [[tokens_z]]
    right, left = tokens_z, tokens_z
    rows = own_rows // 2
    for hop in range(1, half):
        right, left = ring_shift(right, 1), ring_shift(left, -1)
        if hop == 1:
            order = jnp.asarray(ring_order(feat_size), jnp.int32)
            place = jnp.where(feat_at % 2 == 0, feat_at // 2, feat_size - 1 - feat_at // 2)
            keep_mask = keep.astype(F32)
            hops = []
            for away in range(1, half):
                hops += [-away, away]
            hops += [0, half]
            owners = order[(place + jnp.asarray(hops, jnp.int32)) % feat_size]
            keep_ring = keep_mask.reshape(feat_size, own_rows)[owners].reshape(group)
            keep_wide = jnp.broadcast_to(keep_ring[:, None], (group, LANES))
            keep_total = jnp.pad(jnp.sum(keep_mask.reshape(-1, LANES), axis=0), (0, width - LANES))[None]
            right, left, keep_wide, keep_total = together(right, left, keep_wide, keep_total)
        elif hop < half - 1:
            right, left = together(right, left)
        z_stages.append([right, left])
    dec_float = weights[:, 1].astype(F32)
    row_norm = jnp.sqrt(jnp.sum(dec_float * dec_float, axis=(0, 1)))[None]
    near_squares = 0.0
    for hop in range(half - 1):
        for at, piece in enumerate(z_stages[hop]):
            first = group - 2 * own_rows if hop == 0 else (2 * (hop - 1) + at) * own_rows
            kept = keep_wide[first : first + own_rows, :1] * piece.astype(F32) ** 2
            near_squares = near_squares + jnp.sum(kept, axis=0, keepdims=True)
    right, left, weights, row_norm, near_squares = together(right, left, weights, row_norm, near_squares)
    z_stages[half - 1] = [right, left]
    keep_at = [group - 2 * own_rows] + [2 * (hop - 1) * own_rows for hop in range(1, half)] + [group - own_rows]
    acts, recs, stats = [None] * (half + 1), [None] * (half + 1), [None] * (half + 1)
    bias_row = enc_bias[None]

    def encoded(hop, pieces=slice(None)):
        chosen = z_stages[hop][pieces]
        at = keep_at[hop] + (own_rows if pieces == slice(1, 2) else 0)
        act, rec, stat = encode(chosen, keep_wide, at, weights, bias_row)
        if pieces == slice(1, 2):
            act, rec, stat = [*acts[hop], act], [*recs[hop], *rec], [a + b for a, b in zip(stats[hop], stat)]
        elif pieces == slice(0, 1):
            act = [act]
        acts[hop], recs[hop], stats[hop] = act, list(rec), stat

    z_stages.append([ring_shift(right[:rows], 1), ring_shift(left[rows:], -1)])
    encoded(half - 1, slice(0, 1))
    z_stages[half], recs[half - 1], acts[half - 1] = together(z_stages[half], recs[half - 1], acts[half - 1])
    encoded(half)

    recs[half], weights, z_stages[half - 1] = together(recs[half], weights, z_stages[half - 1])
    right, left = recs[half]
    for step in range(1, half + 1):
        right, left = ring_shift(right, 1), ring_shift(left, -1)
        if step == 1:
            encoded(half - 1, slice(1, 2))
            far_squares = [stats[half - 1][2], stats[half][2]]
            right, left, recs[half - 1], acts[half - 1], far_squares = together(
                right, left, recs[half - 1], acts[half - 1], far_squares
            )
        elif step < half:
            hop = half - step
            encoded(hop)
            if step == 2:
                totals = jnp.concatenate([near_squares + far_squares[0] + far_squares[1], keep_total])
                totals = summed(totals, ("dp",))
            right, left, recs[hop], acts[hop], totals = together(right, left, recs[hop], acts[hop], totals)
        else:
            encoded(0)
            right, left, recs[0], acts[0], stats = together(right, left, recs[0], acts[0], stats)
            break
        from_left, from_right = recs[half - step]
        if step == 1:
            right, left = joined(right, left, from_right, from_left)
        else:
            right = (from_right.astype(F32) + right.astype(F32)).astype(BF16)
            left = (from_left.astype(F32) + left.astype(F32)).astype(BF16)
        following = half - step - 1
        right, left, z_stages[following] = together(right, left, z_stages[following])
    own_grad, fit_part, norm_scaled, penalty_scale, counted = compared(
        recs[0][0], right, left, tokens_z, dec_bias[None], keep_wide, keep_at[0], totals, row_norm
    )
    own_grad, fit_part, norm_scaled = together(own_grad, fit_part, norm_scaled)

    wide_by = features // LAST_PARTS
    bias_shares, out_bias_shares = [], []
    carried = middle = None
    middle_biases = []
    grad_stages = [[own_grad]]
    right, left = own_grad, own_grad

    def group_of(plan):
        groups = []
        for hop in plan:
            zs, gs, at = z_stages[hop], grad_stages[hop], keep_at[hop]
            if isinstance(acts[hop], list):
                groups += [(act, [z], [g], at + i * own_rows) for i, (act, z, g) in enumerate(zip(acts[hop], zs, gs))]
            else:
                groups.append((acts[hop], zs, gs, at))
        return groups

    for hop in range(1, half + 1):
        if hop == half:
            right, left = right[:rows], left[rows:]
        right, left = ring_shift(right, 1), ring_shift(left, -1)
        if half - 2 <= hop < half:
            *middle, middle_bias, _ = backward(
                group_of([hop - 1]), keep_wide, norm_scaled, weights, middle or carried, 0, features - wide_by, 0, None
            )
            middle_biases.append(middle_bias)
            right, left, middle = together(right, left, middle)
        elif hop < half:
            *carried, bias_grad, out_bias_grad = backward(
                group_of([hop - 1]), keep_wide, norm_scaled, weights, carried, 0, features, 0, None
            )
            bias_shares.append(bias_grad)
            out_bias_shares.append(out_bias_grad)
            right, left, carried = together(right, left, carried)
        else:
            *ahead, ahead_bias, _ = backward(
                group_of([half - 1]), keep_wide, norm_scaled, weights, middle, 0, wide_by, 0, None
            )
            right, left, ahead, ahead_bias = together(right, left, ahead, ahead_bias)
        grad_stages.append([right, left])

    kept, paired, arrived, last_bias = [], [], [], []
    grads = None

    def crossing(part):
        return [(kept[part][i] + paired[part][i].astype(F32)).astype(BF16) for i in range(1, dp_size // 2)]

    def crossed(part, blocks=None):
        return [swapped(block, "dp", 2 * i + 2) for i, block in enumerate(blocks or crossing(part))]

    def rest_of(block):
        for bit in range(2, dp_size, 2):
            if bit & (bit - 1) == 0:
                block = block + swapped(block, "dp", bit)
        return block

    act_sum, fire_sum, _ = (sum(parts) for parts in zip(*stats))
    counts = jnp.concatenate([fire_sum, act_sum])
    loss_share = LAMBDA * jnp.sum(act_sum * row_norm)
    def last_tokens(part, plan, before):
        keep_part, send_part, bias_grad, out_bias_grad = backward(
            group_of(plan), keep_wide, norm_scaled, weights, before, part * wide_by, wide_by, dp_size, me
        )
        kept.append(keep_part)
        last_bias.append(bias_grad)
        return send_part, out_bias_grad

    counts = counts + swapped(counts, "dp", 1)
    send_part, _ = last_tokens(0, [half], ahead)
    send_part, kept, norm_scaled, counts = together(send_part, kept, norm_scaled, counts)
    counts = rest_of(counts)
    paired.append(swapped(send_part, "dp", 1))
    send_part, _ = last_tokens(1, [half - 1, half], middle)
    send_part, kept, norm_scaled, counts, paired = together(send_part, kept, norm_scaled, counts, paired)
    paired.append(swapped(send_part, "dp", 1))
    blocks = [crossing(0), crossing(1)]
    blocks, kept, norm_scaled, paired = together(blocks, kept, norm_scaled, paired)
    arrived += [crossed(0, blocks[0]), crossed(1, blocks[1])]
    send_part, out_bias_grad = last_tokens(2, [half - 3, half - 2, half - 1, half], carried)
    send_part, kept, arrived, last_bias, out_bias_grad = together(send_part, kept, arrived, last_bias, out_bias_grad)
    paired.append(swapped(send_part, "dp", 1))
    block = crossing(2)
    bias_share = jnp.concatenate([sum(middle_biases) + jnp.concatenate([ahead_bias + last_bias[0], last_bias[1]], axis=1), last_bias[2]], axis=1)
    bias_share = sum(bias_shares) + bias_share
    out_bias_share = jnp.pad(sum(out_bias_shares) + out_bias_grad, ((0, 0), (0, features - width)))
    shares = jnp.concatenate([bias_share, out_bias_share])
    shares = shares + swapped(shares, "dp", 1)
    block, kept, paired, arrived, shares = together(block, kept, paired, arrived, shares)
    fired, act_total = counts[0], counts[1:]
    penalty = penalty_scale * act_total
    shares = rest_of(shares)
    arrived.append(crossed(2, block))
    enc_bias_grad, dec_bias_grad = shares[0], shares[1, :width]
    first_dp = dp_at == 0
    first_both = first_dp & (feat_at == 0)
    bias_squares = jnp.where(first_dp, jnp.sum(enc_bias_grad * enc_bias_grad), 0.0)
    bias_squares = bias_squares + jnp.where(first_both, jnp.sum(dec_bias_grad * dec_bias_grad), 0.0)
    row = lax.broadcasted_iota(jnp.int32, (16, LANES), 0)
    column = lax.broadcasted_iota(jnp.int32, (16, LANES), 1)
    norms = jnp.where((row == 0) & (column == 0), bias_squares, 0.0)
    norms = norms + jnp.where((row == 8) & (column == 0), loss_share, 0.0)
    norms = norms + jnp.pad(fit_part, ((8, 0), (0, 0)))
    for part in range(LAST_PARTS):
        *grads, part_norms = finished(kept[part], paired[part], arrived[part], penalty, both, grads, part)
        norms = norms + part_norms

    norms = summed(norms, everywhere)
    loss_total = jnp.sum(norms[8:])
    overall_derivative_length = jnp.sqrt(jnp.sum(norms[:8]))
    factor = jnp.minimum(1.0, CLIP_NORM / (overall_derivative_length + 1e-06))
    dec_new, dec_m, dec_v = adamw(dec_weight.T, grads[1] * factor, dec_weight_m.T, dec_weight_v.T, DECAY)
    dec_new, dec_m, dec_v = together(dec_new, dec_m, dec_v)
    row_squares = jnp.sum(dec_new * dec_new, axis=0, keepdims=True)
    row_squares = row_squares + swapped(row_squares, "dp", 1)
    enc_grad, row_squares = together(grads[0], row_squares)
    row_squares = rest_of(row_squares)
    enc_new, enc_m, enc_v = adamw(enc_weight, enc_grad * factor, enc_weight_m, enc_weight_v, DECAY)
    bias_new, bias_m, bias_v = adamw(enc_bias, enc_bias_grad * factor, enc_bias_m, enc_bias_v, 0.0)
    out_new, out_m, out_v = adamw(dec_bias, dec_bias_grad * factor, dec_bias_m, dec_bias_v, 0.0)
    dec_new = (dec_new * lax.rsqrt(row_squares + 1e-12)).T
    dec_m, dec_v = dec_m.T, dec_v.T
    return (
        jnp.stack([loss_total, counted[0, 0]]),
        overall_derivative_length,
        fired,
        enc_new,
        enc_m,
        enc_v,
        bias_new,
        bias_m,
        bias_v,
        dec_new,
        dec_m,
        dec_v,
        out_new,
        out_m,
        out_v,
    )


def solution(mesh):
    return jax.shard_map(
        shards,
        mesh=mesh,
        in_specs=(
            P(("dp", "feat"), None),
            P("dp", None),
            P("dp"),
            P(),
            P(),
            P(),
            P(),
            P("dp", "feat"),
            P("feat"),
            P("feat", "dp"),
            P(),
            P("dp", "feat"),
            P("dp", "feat"),
            P("feat"),
            P("feat"),
            P("feat", "dp"),
            P("feat", "dp"),
            P(),
            P(),
        ),
        out_specs=(
            P(),
            P(),
            P("feat"),
            P("dp", "feat"),
            P("dp", "feat"),
            P("dp", "feat"),
            P("feat"),
            P("feat"),
            P("feat"),
            P("feat", "dp"),
            P("feat", "dp"),
            P("feat", "dp"),
            P(),
            P(),
            P(),
        ),
        check_vma=False,
    )
```

```python
import functools
import math

import jax
import jax.numpy as jnp
from jax import lax
from jax.experimental import pallas as pl
from jax.experimental.pallas import tpu as pltpu
from jax.sharding import PartitionSpec as P

HEAD = 64
ROW_LEN = 1024
CTX = 128
STEP = 10

LAMBDA = 0.001
CLIP_NORM = 0.004
LEARN = 0.02
BETA_ONE = 0.9
BETA_TWO = 0.999
EPSILON = 1e-08
DECAY = 0.01

ENCODE_BLOCK = 768
BACKWARD_BLOCK = 512
ROW_BLOCK = 512
LANES = 128
VMEM_BYTES = 60 * 2**20
SMALL_VMEM_BYTES = 24 * 2**20
LAST_PARTS = 3
PACK_BLOCK = 1536
COST_SHARE = 4
BF16 = jnp.bfloat16
F32 = jnp.float32


def kernel_params(size=None):
    return pltpu.CompilerParams(vmem_limit_bytes=size or VMEM_BYTES)


def dot_nn(a, b):
    return jnp.dot(a, b, preferred_element_type=F32)


def dot_nt(a, b):
    return lax.dot_general(a, b, (((1,), (1,)), ((), ())), preferred_element_type=F32)


def dot_tn(a, b):
    return lax.dot_general(a, b, (((0,), (0,)), ((), ())), preferred_element_type=F32)


def together(*values):
    leaves, tree = jax.tree.flatten(values)
    return jax.tree.unflatten(tree, lax.optimization_barrier(tuple(leaves)))


def normed(block, gain, shift):
    values = block.astype(F32)
    centred = values - jnp.mean(values, axis=1, keepdims=True)
    variance = jnp.mean(centred * centred, axis=1, keepdims=True)
    return (centred * lax.rsqrt(variance + 1e-05) * gain + shift).astype(BF16)


def project_kernel(rows_ref, gain_ref, bias_ref, w_ref, wb_ref, out_ref, w_s, sem):
    width = rows_ref.shape[1]
    loads = []
    for block in range(3):
        load = pltpu.make_async_copy(w_ref.at[:, pl.ds(block * width, width)], w_s.at[block], sem.at[block])
        load.start()
        loads.append(load)
    gain = gain_ref[...].astype(F32).reshape(1, width)
    shift = bias_ref[...].astype(F32).reshape(1, width)
    offsets = wb_ref[...].astype(F32).reshape(1, 3 * width)
    rows = normed(rows_ref[...], gain, shift)
    for block, load in enumerate(loads):
        columns = slice(block * width, (block + 1) * width)
        load.wait()
        out_ref[:, columns] = (dot_nn(rows, w_s[block]) + offsets[:, columns]).astype(BF16)


def project(resid, ln_gain, ln_bias, qkv_weight, qkv_bias):
    rows, width = resid.shape
    vmem = pl.BlockSpec(memory_space=pltpu.VMEM)
    return pl.pallas_call(
        project_kernel,
        in_specs=[vmem] * 3 + [pl.BlockSpec(memory_space=pl.ANY), vmem],
        out_specs=vmem,
        out_shape=jax.ShapeDtypeStruct((rows, 3 * width), BF16),
        scratch_shapes=[pltpu.VMEM((3, width, width), BF16), pltpu.SemaphoreType.DMA((3,))],
        compiler_params=kernel_params(),
        cost_estimate=pl.CostEstimate(flops=6 * rows * width * width, bytes_accessed=6 * width * width, transcendentals=0),
        name="project",
    )(resid, ln_gain, ln_bias, qkv_weight, qkv_bias)


def attend_kernel(own_ref, tail_ref, seg_q_ref, seg_k_ref, gain_ref, bias_ref, w_ref, wb_ref, z_ref, w_s, kv_s, sem):
    rows, width = z_ref.shape
    load = pltpu.make_async_copy(w_ref.at[:, pl.ds(width, 2 * width)], w_s, sem)
    load.start()
    lane = lax.broadcasted_iota(jnp.int32, (CTX, 2 * HEAD), 1)
    first_head = lane < HEAD
    place_q = lax.broadcasted_iota(jnp.int32, (CTX, 2 * CTX), 0) + CTX
    place_k = lax.broadcasted_iota(jnp.int32, (CTX, 2 * CTX), 1)
    earlier = place_k <= place_q

    def pairs_of(block, columns):
        if block > 0:
            return own_ref[(block - 1) * CTX : (block + 1) * CTX, columns]
        return jnp.concatenate([kv_s[:, columns.start - width : columns.stop - width], own_ref[:CTX, columns]], axis=0)

    for block in (*range(1, rows // CTX), 0):
        if block == 0:
            load.wait()
            gain = gain_ref[...].astype(F32).reshape(1, width)
            shift = bias_ref[...].astype(F32).reshape(1, width)
            offsets = wb_ref[...].astype(F32).reshape(1, 3 * width)
            tail = normed(tail_ref[...], gain, shift)
            kv_s[...] = (dot_nn(tail, w_s[...]) + offsets[:, width:]).astype(BF16)
        base = block * CTX
        seg_q = seg_q_ref[base : base + CTX, :]
        allowed = (jnp.concatenate([seg_q, seg_q], axis=1) == seg_k_ref[:, base : base + 2 * CTX]) & earlier
        allowed = jnp.concatenate([allowed, allowed], axis=0)
        starts = range(0, width, 2 * HEAD)
        scores = []
        for start in starts:
            query = own_ref[base : base + CTX, start : start + 2 * HEAD]
            keys = pairs_of(block, slice(width + start, width + start + 2 * HEAD))
            none = jnp.zeros_like(query)
            query = query * jnp.asarray(1.0 / math.sqrt(HEAD), BF16)
            query = jnp.concatenate([jnp.where(first_head, query, none), jnp.where(first_head, none, query)], axis=0)
            scores.append(dot_nt(query, keys))
        probs = []
        for part in scores:
            part = jnp.where(allowed, part, -1e30)
            expo = jnp.exp(part - jnp.max(part, axis=1, keepdims=True))
            probs.append((expo * (1.0 / jnp.sum(expo, axis=1, keepdims=True))).astype(BF16))
        for start, part in zip(starts, probs):
            values = pairs_of(block, slice(2 * width + start, 2 * width + start + 2 * HEAD))
            mixed = dot_nn(part, values)
            z_ref[base : base + CTX, start : start + 2 * HEAD] = jnp.where(first_head, mixed[:CTX], mixed[CTX:]).astype(BF16)


def attend(projected, tail, seg_q, seg_k, ln_gain, ln_bias, qkv_weight, qkv_bias):
    rows = projected.shape[0]
    width = tail.shape[1]
    vmem = pl.BlockSpec(memory_space=pltpu.VMEM)
    return pl.pallas_call(
        attend_kernel,
        in_specs=[vmem] * 6 + [pl.BlockSpec(memory_space=pl.ANY), vmem],
        out_specs=vmem,
        out_shape=jax.ShapeDtypeStruct((rows, width), BF16),
        scratch_shapes=[
            pltpu.VMEM((width, 2 * width), BF16),
            pltpu.VMEM((CTX, 2 * width), BF16),
            pltpu.SemaphoreType.DMA,
        ],
        compiler_params=kernel_params(),
        cost_estimate=pl.CostEstimate(
            flops=4 * rows * width * width, bytes_accessed=8 * width * width, transcendentals=rows * 2 * CTX * 12
        ),
        name="attend",
    )(projected, tail, seg_q, seg_k, ln_gain, ln_bias, qkv_weight, qkv_bias)


def packed_kernel(enc_ref, dec_ref, out_ref):
    out_ref[0] = enc_ref[...].astype(BF16)
    out_ref[1] = dec_ref[...].astype(BF16)


def packed(enc, dec):
    rows, columns = enc.shape
    block = PACK_BLOCK
    across = lambda j: (0, j)
    return pl.pallas_call(
        packed_kernel,
        grid=(columns // block,),
        in_specs=[pl.BlockSpec((rows, block), across)] * 2,
        out_specs=pl.BlockSpec((2, rows, block), lambda j: (0, 0, j)),
        out_shape=jax.ShapeDtypeStruct((2, rows, columns), BF16),
        compiler_params=kernel_params(),
        cost_estimate=pl.CostEstimate(flops=0, bytes_accessed=12 * rows * columns, transcendentals=0),
        name="packed",
    )(enc, dec)


def encode_kernel(count, *refs):
    z_refs, (keep_ref, enc_ref, bias_ref, dec_ref), rest = refs[:count], refs[count : count + 4], refs[count + 4 :]
    act_ref, rec_refs, (sum_ref, fire_ref, square_ref) = rest[0], rest[1 : 1 + count], rest[1 + count : 4 + count]
    totals = rest[4 + count :]
    step, last = pl.program_id(0), pl.num_programs(0) - 1
    features = enc_ref.shape[-1]

    def whole(ref):
        return ref[...].reshape(-1, features)

    @pl.when(step == 0)
    def _():
        spot, squares = 0, 0.0
        for total, z_ref in zip(totals, z_refs):
            total[...] = jnp.zeros_like(total)
            size, width = z_ref.shape
            values = z_ref[...].astype(F32)
            kept = wide(keep_ref[spot : spot + size, :], width) * values * values
            squares = squares + jnp.sum(kept.reshape(-1, 8, width), axis=0)
            spot += size
        square_ref[...] = jnp.sum(squares, axis=0, keepdims=True)

    blocks, spot = [], 0
    for piece in range(count):
        size = z_refs[piece].shape[0]
        block = min(ROW_BLOCK, size)
        for base in range(0, size, block):
            blocks.append((piece, slice(base, base + block), slice(spot + base, spot + base + block)))
        spot += size

    def preact_of(piece, rows):
        return dot_nn(z_refs[piece][rows, :], whole(enc_ref)) + bias_ref[...]

    sums = jnp.zeros((8, features), F32)
    fires = jnp.zeros((8, features), F32)
    coming = preact_of(*blocks[0][:2])
    for at, (piece, rows, place) in enumerate(blocks):
        preact = coming
        if at + 1 < len(blocks):
            coming = preact_of(*blocks[at + 1][:2])
        tiny = jnp.exp(-jnp.abs(preact))
        log_part = jnp.where(tiny < 2.0**-10, tiny * (1.0 - 0.5 * tiny), jnp.log(1.0 + tiny))
        act = jnp.maximum(preact, 0.0) + log_part
        low = act.astype(BF16)
        act_ref[place, :] = low
        kept = wide(keep_ref[place, :], features) * act
        sums = sums + jnp.sum(kept.reshape(-1, 8, features), axis=0)
        fires = fires + jnp.sum(jnp.tanh(kept).reshape(-1, 8, features), axis=0)
        totals[piece][rows, :] += dot_nt(low, whole(dec_ref))
    sum_ref[...] = jnp.sum(sums, axis=0, keepdims=True)
    fire_ref[...] = jnp.sum(fires, axis=0, keepdims=True)

    @pl.when(step == last)
    def _():
        for piece in range(count):
            rec_refs[piece][...] = totals[piece][...].astype(BF16)


def wide(block, columns):
    return jnp.concatenate([block] * (columns // block.shape[1]), axis=1)


def encode(pieces, keep_wide, keep_at, weights, bias):
    parts, _, rows, features = weights.shape
    width = parts * rows
    sizes = [p.shape[0] for p in pieces]
    tokens = sum(sizes)
    fb = ENCODE_BLOCK
    whole = lambda j: (0, 0)
    across = lambda j: (0, j)
    keep_block = keep_at // tokens
    outs = pl.pallas_call(
        functools.partial(encode_kernel, len(pieces)),
        grid=(features // fb,),
        in_specs=[pl.BlockSpec((s, width), whole) for s in sizes]
        + [
            pl.BlockSpec((tokens, LANES), lambda j: (keep_block, 0)),
            pl.BlockSpec((parts, None, rows, fb), lambda j: (0, 0, 0, j)),
            pl.BlockSpec((1, fb), across),
            pl.BlockSpec((parts, None, rows, fb), lambda j: (0, 1, 0, j)),
        ],
        out_specs=[pl.BlockSpec((tokens, fb), across)]
        + [pl.BlockSpec((s, width), whole) for s in sizes]
        + [pl.BlockSpec((1, fb), across)] * 2
        + [pl.BlockSpec((1, width), whole)],
        out_shape=[jax.ShapeDtypeStruct((tokens, features), BF16)]
        + [jax.ShapeDtypeStruct((s, width), BF16) for s in sizes]
        + [jax.ShapeDtypeStruct((1, features), F32)] * 2
        + [jax.ShapeDtypeStruct((1, width), F32)],
        scratch_shapes=[pltpu.VMEM((s, width), F32) for s in sizes],
        compiler_params=kernel_params(),
        cost_estimate=pl.CostEstimate(
            flops=4 * tokens * width * features // COST_SHARE,
            bytes_accessed=2 * (2 * width * features + tokens * (features + 4 * width)) // COST_SHARE,
            transcendentals=3 * tokens * features // COST_SHARE,
        ),
        name="encode",
    )(*pieces, keep_wide, weights, bias, weights)
    return outs[0], outs[1 : 1 + len(pieces)], outs[-3:]


def joined_kernel(right_ref, left_ref, from_right_ref, from_left_ref, right_out, left_out):
    rows = right_ref.shape[0]
    right_out[:rows, :] = (from_right_ref[:rows, :].astype(F32) + right_ref[...].astype(F32)).astype(BF16)
    right_out[rows:, :] = from_right_ref[rows:, :]
    left_out[:rows, :] = from_left_ref[:rows, :]
    left_out[rows:, :] = (from_left_ref[rows:, :].astype(F32) + left_ref[...].astype(F32)).astype(BF16)


def joined(right, left, from_right, from_left):
    rows, width = from_right.shape
    half = pl.BlockSpec((rows // 2, 2 * LANES), lambda j: (0, j))
    full = pl.BlockSpec((rows, 2 * LANES), lambda j: (0, j))
    return pl.pallas_call(
        joined_kernel,
        grid=(width // (2 * LANES),),
        in_specs=[half, half, full, full],
        out_specs=[full, full],
        out_shape=[jax.ShapeDtypeStruct((rows, width), BF16)] * 2,
        compiler_params=kernel_params(SMALL_VMEM_BYTES),
        name="joined",
    )(right, left, from_right, from_left)


def compared_kernel(rec_ref, right_ref, left_ref, z_ref, bias_ref, keep_ref, totals_ref, norm_ref, grad_ref, fit_ref, scaled_ref, penalty_ref, counted_ref):
    rows, width = z_ref.shape
    squares = jnp.sum(totals_ref[0:1, :], keepdims=True)
    counted = jnp.sum(totals_ref[1:2, :], keepdims=True)
    mean_square = squares / (counted * width) + 1e-06
    unit = 2.0 / (width * mean_square * counted)
    residue = rec_ref[...].astype(F32) + right_ref[...].astype(F32) + left_ref[...].astype(F32)
    residue = residue + bias_ref[...] - z_ref[...].astype(F32)
    kept = wide(keep_ref[...], width) * residue
    grad_ref[...] = (kept * unit).astype(BF16)
    fit = jnp.sum((kept * residue).reshape(rows // 8, 8, width), axis=0)

    @pl.when(pl.program_id(0) == 0)
    def _():
        share = LAMBDA / counted
        norms = norm_ref[...]
        scaled_ref[...] = share * norms
        penalty_ref[...] = share / norms
        counted_ref[...] = counted + jnp.zeros(counted_ref.shape, F32)
        fit_ref[...] = jnp.zeros_like(fit_ref)

    fit_ref[...] += sum(fit[:, at : at + LANES] for at in range(0, width, LANES)) / (width * mean_square)


def compared(rec, right, left, tokens_z, dec_bias, keep_wide, keep_at, totals, row_norm):
    rows, width = tokens_z.shape
    features = row_norm.shape[1]
    block = CTX
    whole = lambda j: (0, 0)
    own = pl.BlockSpec((block, width), lambda j: (j, 0))
    line = pl.BlockSpec((1, features), whole)
    tile = pl.BlockSpec((8, LANES), whole)
    return pl.pallas_call(
        compared_kernel,
        grid=(rows // block,),
        in_specs=[own] * 4
        + [
            pl.BlockSpec((1, width), whole),
            pl.BlockSpec((block, LANES), lambda j: (keep_at // block + j, 0)),
            pl.BlockSpec(totals.shape, whole),
            line,
        ],
        out_specs=[own, tile, line, line, tile],
        out_shape=[
            jax.ShapeDtypeStruct((rows, width), BF16),
            jax.ShapeDtypeStruct((8, LANES), F32),
            jax.ShapeDtypeStruct((1, features), F32),
            jax.ShapeDtypeStruct((1, features), F32),
            jax.ShapeDtypeStruct((8, LANES), F32),
        ],
        compiler_params=kernel_params(),
        name="compared",
    )(rec, right, left, tokens_z, dec_bias, keep_wide, totals, row_norm)


def backward_kernel(groups, carried, parted, *refs):
    refs = list(refs)
    slots = refs.pop(0) if parted else None
    acts, zs, gs, keeps = [], [], [], []
    for count in groups:
        acts.append(refs.pop(0))
        zs.append([refs.pop(0) for _ in range(count)])
        gs.append([refs.pop(0) for _ in range(count)])
        keeps.append(refs.pop(0))
    norm_ref, dec_ref = refs.pop(0), refs.pop(0)
    enc_in, dec_in = (refs.pop(0), refs.pop(0)) if carried else (None, None)
    outs = [refs.pop(0) for _ in range(2)]
    bias_ref, out_bias_ref, pre_s = refs
    features = dec_ref.shape[-1]

    @pl.when(pl.program_id(0) == 0)
    def _():
        total = 0.0
        for g_list in gs:
            for g_ref in g_list:
                total = total + jnp.sum(g_ref[...].astype(F32).reshape(-1, 8, g_ref.shape[1]), axis=0)
        out_bias_ref[...] = jnp.sum(total, axis=0, keepdims=True)


    blocks, pieces, spot = [], [], 0
    for act_ref, z_list, g_list, keep_ref in zip(acts, zs, gs, keeps):
        at = 0
        for z_ref, g_ref in zip(z_list, g_list):
            size = g_ref.shape[0]
            block = min(ROW_BLOCK, size)
            for base in range(0, size, block):
                blocks.append((g_ref, slice(base, base + block), act_ref, keep_ref, slice(at + base, at + base + block), slice(spot + base, spot + base + block)))
            pieces.append((z_ref, g_ref, act_ref, slice(at, at + size), slice(spot, spot + size)))
            at += size
            spot += size

    def grad_of(g_ref, rows):
        return dot_nn(g_ref[rows, :], dec_ref[...].reshape(-1, features))

    sums = jnp.zeros((8, features), F32)
    coming = grad_of(*blocks[0][:2])
    for at, (_, _, act_ref, keep_ref, local, place) in enumerate(blocks):
        grad_act = coming
        if at + 1 < len(blocks):
            coming = grad_of(*blocks[at + 1][:2])
        act = act_ref[local, :].astype(F32)
        slope = jnp.where(act < 2.0**-10, act * (1.0 - 0.5 * act), 1.0 - jnp.exp(-act))
        pre = (grad_act + wide(keep_ref[local, :], features) * norm_ref[...]) * slope
        sums = sums + jnp.sum(pre.reshape(-1, 8, features), axis=0)
        pre_s[place, :] = pre.astype(BF16)
    bias_ref[...] = jnp.sum(sums, axis=0, keepdims=True)
    dec_part = dec_in[...] if carried else None
    for _, g_ref, act_ref, local, _ in pieces:
        term = dot_tn(g_ref[...], act_ref[local, :])
        dec_part = term if dec_part is None else dec_part + term
    enc_part = enc_in[...] if carried else None
    for z_ref, _, _, _, place in pieces:
        term = dot_tn(z_ref[...], pre_s[place, :])
        enc_part = term if enc_part is None else enc_part + term
    if not parted:
        outs[0][...] = enc_part
        outs[1][...] = dec_part
        return
    keep_out, send_out = outs
    me = slots[0]
    for matrix, value in enumerate((enc_part, dec_part)):
        rows = value.shape[0] // parted
        for owner in range(parted):
            away = owner ^ me
            half = away // 2
            piece = value[owner * rows : (owner + 1) * rows, :]

            @pl.when(away % 2 == 0)
            def _():
                keep_out[pl.ds(half, 1), matrix] = piece[None]

            @pl.when(away % 2 == 1)
            def _():
                send_out[pl.ds(half, 1), matrix] = piece[None].astype(send_out.dtype)


def backward(groups, keep_wide, norm_scaled, weights, carried, first, wide_by, parted, me):
    blocks, _, rows, _ = weights.shape
    width = blocks * rows
    counts = [len(zs) for _, zs, _, _ in groups]
    tokens = sum(act.shape[0] for act, _, _, _ in groups)
    fb = BACKWARD_BLOCK
    start = first // fb
    whole = lambda j, *_: (0, 0)
    across = lambda j, *_: (0, j + start)
    local = lambda j, *_: (0, j)
    operands, specs = [], []
    for act, zs, gs, keep_at in groups:
        size = act.shape[0]
        operands.append(act)
        specs.append(pl.BlockSpec((size, fb), across))
        for piece in (*zs, *gs):
            operands.append(piece)
            specs.append(pl.BlockSpec(piece.shape, whole, pipeline_mode=pl.Buffered(1)))
        operands.append(keep_wide)
        specs.append(pl.BlockSpec((size, LANES), lambda j, *_, at=keep_at // size: (at, 0)))
    operands += [norm_scaled, weights]
    specs += [pl.BlockSpec((1, fb), across), pl.BlockSpec((blocks, None, rows, fb), lambda j, *_: (0, 1, 0, j + start))]
    if carried is not None:
        operands += list(carried)
        specs += [pl.BlockSpec((width, fb), across)] * 2
    if parted:
        shape = (parted // 2, 2, width // parted, wide_by)
        block = pl.BlockSpec((parted // 2, 2, width // parted, fb), lambda j, *_: (0, 0, 0, j))
        out_shape = [jax.ShapeDtypeStruct(shape, F32), jax.ShapeDtypeStruct(shape, BF16)]
        out_specs = [block] * 2
    else:
        out_shape = [jax.ShapeDtypeStruct((width, wide_by), F32)] * 2
        out_specs = [pl.BlockSpec((width, fb), local)] * 2
    out_shape += [jax.ShapeDtypeStruct((1, wide_by), F32), jax.ShapeDtypeStruct((1, width), F32)]
    out_specs += [pl.BlockSpec((1, fb), local), pl.BlockSpec((1, width), whole)]
    return pl.pallas_call(
        functools.partial(backward_kernel, counts, carried is not None, parted),
        grid_spec=pltpu.PrefetchScalarGridSpec(
            num_scalar_prefetch=1 if parted else 0,
            grid=(wide_by // fb,),
            in_specs=specs,
            out_specs=out_specs,
            scratch_shapes=[pltpu.VMEM((tokens, fb), BF16)],
        ),
        out_shape=out_shape,
        compiler_params=kernel_params(),
        cost_estimate=pl.CostEstimate(
            flops=6 * tokens * width * wide_by // COST_SHARE,
            bytes_accessed=(2 * tokens * wide_by + 16 * width * wide_by) // COST_SHARE,
            transcendentals=tokens * wide_by // COST_SHARE,
        ),
        name="backward",
    )(*([me] if parted else []), *operands)


def finished_kernel(arrived_count, first, kept_ref, paired_ref, *refs):
    arrived, (penalty_ref, low_ref), rest = refs[:arrived_count], refs[arrived_count : arrived_count + 2], refs[arrived_count + 2 :]
    enc_ref, dec_ref, norm_ref = rest if first else rest[2:]
    grad = kept_ref[...] + paired_ref[...].astype(F32)
    for block in arrived:
        grad = grad + block[...].astype(F32)
    enc, dec = grad[0], grad[1] + penalty_ref[...] * low_ref[...].astype(F32)
    enc_ref[...] = enc
    dec_ref[...] = dec
    squares = enc * enc + dec * dec
    total = jnp.sum(squares.reshape(-1, 8, squares.shape[1]), axis=0)
    lanes = sum(total[:, at : at + LANES] for at in range(0, total.shape[1], LANES))

    @pl.when(pl.program_id(0) == 0)
    def _():
        norm_ref[...] = jnp.zeros_like(norm_ref)

    norm_ref[:8, :] += lanes


def finished(kept, paired, arrived, penalty, both, grads, part):
    _, _, rows, wide_by = kept.shape
    features = both.shape[2]
    fb = BACKWARD_BLOCK
    start = part * wide_by // fb
    own = pl.BlockSpec((None, 2, rows, fb), lambda j: (0, 0, 0, j))
    along = pl.BlockSpec((2, rows, fb), lambda j: (0, 0, j))
    first = grads is None
    return pl.pallas_call(
        functools.partial(finished_kernel, len(arrived), first),
        grid=(wide_by // fb,),
        in_specs=[own, own]
        + [along] * len(arrived)
        + [
            pl.BlockSpec((1, fb), lambda j: (0, j + start)),
            pl.BlockSpec((None, rows, fb), lambda j: (1, 0, j + start)),
        ]
        + ([] if first else [pl.BlockSpec(memory_space=pl.ANY)] * 2),
        out_specs=[pl.BlockSpec((rows, fb), lambda j: (0, j + start))] * 2 + [pl.BlockSpec((16, LANES), lambda j: (0, 0))],
        out_shape=[jax.ShapeDtypeStruct((rows, features), F32)] * 2 + [jax.ShapeDtypeStruct((16, LANES), F32)],
        input_output_aliases={} if first else {4 + len(arrived): 0, 5 + len(arrived): 1},
        compiler_params=kernel_params(),
        cost_estimate=pl.CostEstimate(flops=0, bytes_accessed=24 * rows * wide_by, transcendentals=0),
        name="finished",
    )(kept, paired, *arrived, penalty, both, *([] if first else grads))


def ring_order(count):
    return list(range(0, count, 2)) + list(range(1, count, 2))[::-1]


def ring_shift(block, direction):
    order = ring_order(lax.axis_size("feat"))
    count = len(order)
    route = [(order[i], order[(i + direction) % count]) for i in range(count)]
    return lax.ppermute(block, "feat", route)


def swapped(block, axis, bit):
    return lax.ppermute(block, axis, [(i, i ^ bit) for i in range(lax.axis_size(axis))])


def summed(block, axes):
    for axis in axes:
        size, bit = lax.axis_size(axis), 1
        while bit < size:
            block = block + swapped(block, axis, bit)
            bit *= 2
    return block


def adamw(weight, grad, first, second, decay):
    first = BETA_ONE * first + (1.0 - BETA_ONE) * grad
    second = BETA_TWO * second + (1.0 - BETA_TWO) * grad * grad
    hat_first = first / (1.0 - BETA_ONE**STEP)
    hat_second = second / (1.0 - BETA_TWO**STEP)
    weight = weight - LEARN * (hat_first / (jnp.sqrt(hat_second) + EPSILON) + decay * weight)
    return (weight, first, second)


def shards(
    resid,
    segments,
    keep,
    ln_gain,
    ln_bias,
    qkv_weight,
    qkv_bias,
    enc_weight,
    enc_bias,
    dec_weight,
    dec_bias,
    enc_weight_m,
    enc_weight_v,
    enc_bias_m,
    enc_bias_v,
    dec_weight_m,
    dec_weight_v,
    dec_bias_m,
    dec_bias_v,
):
    own_rows, width = resid.shape
    group = keep.shape[0]
    feat_size, dp_size = lax.axis_size("feat"), lax.axis_size("dp")
    half = feat_size // 2
    features = enc_weight.shape[1]
    feat_at, dp_at = lax.axis_index("feat"), lax.axis_index("dp")
    everywhere = ("dp", "feat")

    me = dp_at.reshape(1).astype(jnp.int32)

    offset = feat_at * own_rows
    row_ids = jnp.arange(group, dtype=jnp.int32)
    seg_all = segments.reshape(group) + row_ids // ROW_LEN * ROW_LEN
    own_seg = lax.dynamic_slice_in_dim(seg_all, offset, own_rows)
    tail_seg = lax.dynamic_slice_in_dim(seg_all, jnp.maximum(offset - CTX, 0), CTX)
    tail_seg = jnp.where(feat_at > 0, tail_seg, -1)
    key_seg = jnp.concatenate([tail_seg, own_seg])[None]
    seg_wide = jnp.broadcast_to(own_seg[:, None], (own_rows, LANES))
    both = packed(enc_weight, dec_weight.T)
    weights = lax.all_gather(both, "dp")
    tail = lax.ppermute(resid[own_rows - CTX :], "feat", [(i, (i + 1) % feat_size) for i in range(feat_size)])
    projected = project(resid, ln_gain, ln_bias, qkv_weight, qkv_bias)
    tail, key_seg, seg_wide, both, projected = together(tail, key_seg, seg_wide, both, projected)
    tokens_z = attend(projected, tail, seg_wide, key_seg, ln_gain, ln_bias, qkv_weight, qkv_bias)
    tokens_z, keep = together(tokens_z, keep)

    z_stages = [[tokens_z]]
    right, left = tokens_z, tokens_z
    rows = own_rows // 2
    for hop in range(1, half):
        right, left = ring_shift(right, 1), ring_shift(left, -1)
        if hop == 1:
            order = jnp.asarray(ring_order(feat_size), jnp.int32)
            place = jnp.where(feat_at % 2 == 0, feat_at // 2, feat_size - 1 - feat_at // 2)
            keep_mask = keep.astype(F32)
            hops = []
            for away in range(1, half):
                hops += [-away, away]
            hops += [0, half]
            owners = order[(place + jnp.asarray(hops, jnp.int32)) % feat_size]
            keep_ring = keep_mask.reshape(feat_size, own_rows)[owners].reshape(group)
            keep_wide = jnp.broadcast_to(keep_ring[:, None], (group, LANES))
            keep_total = jnp.pad(jnp.sum(keep_mask.reshape(-1, LANES), axis=0), (0, width - LANES))[None]
            right, left, keep_wide, keep_total = together(right, left, keep_wide, keep_total)
        elif hop < half - 1:
            right, left = together(right, left)
        z_stages.append([right, left])
    dec_float = weights[:, 1].astype(F32)
    row_norm = jnp.sqrt(jnp.sum(dec_float * dec_float, axis=(0, 1)))[None]
    near_squares = 0.0
    for hop in range(half - 1):
        for at, piece in enumerate(z_stages[hop]):
            first = group - 2 * own_rows if hop == 0 else (2 * (hop - 1) + at) * own_rows
            kept = keep_wide[first : first + own_rows, :1] * piece.astype(F32) ** 2
            near_squares = near_squares + jnp.sum(kept, axis=0, keepdims=True)
    right, left, weights, row_norm, near_squares = together(right, left, weights, row_norm, near_squares)
    z_stages[half - 1] = [right, left]
    keep_at = [group - 2 * own_rows] + [2 * (hop - 1) * own_rows for hop in range(1, half)] + [group - own_rows]
    acts, recs, stats = [None] * (half + 1), [None] * (half + 1), [None] * (half + 1)
    bias_row = enc_bias[None]

    def encoded(hop, pieces=slice(None)):
        chosen = z_stages[hop][pieces]
        at = keep_at[hop] + (own_rows if pieces == slice(1, 2) else 0)
        act, rec, stat = encode(chosen, keep_wide, at, weights, bias_row)
        if pieces == slice(1, 2):
            act, rec, stat = [*acts[hop], act], [*recs[hop], *rec], [a + b for a, b in zip(stats[hop], stat)]
        elif pieces == slice(0, 1):
            act = [act]
        acts[hop], recs[hop], stats[hop] = act, list(rec), stat

    z_stages.append([ring_shift(right[:rows], 1), ring_shift(left[rows:], -1)])
    encoded(half - 1, slice(0, 1))
    z_stages[half], recs[half - 1], acts[half - 1] = together(z_stages[half], recs[half - 1], acts[half - 1])
    encoded(half)

    recs[half], weights, z_stages[half - 1] = together(recs[half], weights, z_stages[half - 1])
    right, left = recs[half]
    for step in range(1, half + 1):
        right, left = ring_shift(right, 1), ring_shift(left, -1)
        if step == 1:
            encoded(half - 1, slice(1, 2))
            right, left, recs[half - 1], acts[half - 1] = together(right, left, recs[half - 1], acts[half - 1])
        elif step < half:
            hop = half - step
            encoded(hop)
            right, left, recs[hop], acts[hop], stats = together(right, left, recs[hop], acts[hop], stats)
        else:
            totals = summed(jnp.concatenate([near_squares + stats[half - 1][2] + stats[half][2], keep_total]), ("dp",))
            encoded(0)
            right, left, recs[0], acts[0], stats, totals = together(right, left, recs[0], acts[0], stats, totals)
            break
        from_left, from_right = recs[half - step]
        if step == 1:
            right, left = joined(right, left, from_right, from_left)
        else:
            right = (from_right.astype(F32) + right.astype(F32)).astype(BF16)
            left = (from_left.astype(F32) + left.astype(F32)).astype(BF16)
        following = half - step - 1
        right, left, z_stages[following] = together(right, left, z_stages[following])
    own_grad, fit_part, norm_scaled, penalty_scale, counted = compared(
        recs[0][0], right, left, tokens_z, dec_bias[None], keep_wide, keep_at[0], totals, row_norm
    )
    own_grad, fit_part, norm_scaled = together(own_grad, fit_part, norm_scaled)

    wide_by = features // LAST_PARTS
    bias_shares, out_bias_shares = [], []
    carried = middle = None
    middle_biases = []
    grad_stages = [[own_grad]]
    right, left = own_grad, own_grad

    def group_of(plan):
        groups = []
        for hop in plan:
            zs, gs, at = z_stages[hop], grad_stages[hop], keep_at[hop]
            if isinstance(acts[hop], list):
                groups += [(act, [z], [g], at + i * own_rows) for i, (act, z, g) in enumerate(zip(acts[hop], zs, gs))]
            else:
                groups.append((acts[hop], zs, gs, at))
        return groups

    for hop in range(1, half + 1):
        if hop == half:
            right, left = right[:rows], left[rows:]
        right, left = ring_shift(right, 1), ring_shift(left, -1)
        if half - 2 <= hop < half:
            *middle, middle_bias, _ = backward(
                group_of([hop - 1]), keep_wide, norm_scaled, weights, middle or carried, 0, features - wide_by, 0, None
            )
            middle_biases.append(middle_bias)
            right, left, middle = together(right, left, middle)
        elif hop < half:
            *carried, bias_grad, out_bias_grad = backward(
                group_of([hop - 1]), keep_wide, norm_scaled, weights, carried, 0, features, 0, None
            )
            bias_shares.append(bias_grad)
            out_bias_shares.append(out_bias_grad)
            right, left, carried = together(right, left, carried)
        else:
            *ahead, ahead_bias, _ = backward(
                group_of([half - 1]), keep_wide, norm_scaled, weights, middle, 0, wide_by, 0, None
            )
            right, left, ahead, ahead_bias = together(right, left, ahead, ahead_bias)
        grad_stages.append([right, left])

    kept, paired, arrived, last_bias = [], [], [], []
    grads = None

    def crossing(part):
        return [(kept[part][i] + paired[part][i].astype(F32)).astype(BF16) for i in range(1, dp_size // 2)]

    def crossed(part, blocks=None):
        return [swapped(block, "dp", 2 * i + 2) for i, block in enumerate(blocks or crossing(part))]

    def rest_of(block):
        for bit in range(2, dp_size, 2):
            if bit & (bit - 1) == 0:
                block = block + swapped(block, "dp", bit)
        return block

    act_sum, fire_sum, _ = (sum(parts) for parts in zip(*stats))
    counts = jnp.concatenate([fire_sum, act_sum])
    loss_share = LAMBDA * jnp.sum(act_sum * row_norm)
    def last_tokens(part, plan, before):
        keep_part, send_part, bias_grad, out_bias_grad = backward(
            group_of(plan), keep_wide, norm_scaled, weights, before, part * wide_by, wide_by, dp_size, me
        )
        kept.append(keep_part)
        last_bias.append(bias_grad)
        return send_part, out_bias_grad

    counts = counts + swapped(counts, "dp", 1)
    send_part, _ = last_tokens(0, [half], ahead)
    send_part, kept, norm_scaled, counts = together(send_part, kept, norm_scaled, counts)
    counts = rest_of(counts)
    paired.append(swapped(send_part, "dp", 1))
    send_part, _ = last_tokens(1, [half - 1, half], middle)
    send_part, kept, norm_scaled, counts, paired = together(send_part, kept, norm_scaled, counts, paired)
    paired.append(swapped(send_part, "dp", 1))
    blocks = [crossing(0), crossing(1)]
    blocks, kept, norm_scaled, paired = together(blocks, kept, norm_scaled, paired)
    arrived += [crossed(0, blocks[0]), crossed(1, blocks[1])]
    send_part, out_bias_grad = last_tokens(2, [half - 3, half - 2, half - 1, half], carried)
    send_part, kept, arrived, last_bias, out_bias_grad = together(send_part, kept, arrived, last_bias, out_bias_grad)
    paired.append(swapped(send_part, "dp", 1))
    block = crossing(2)
    bias_share = jnp.concatenate([sum(middle_biases) + jnp.concatenate([ahead_bias + last_bias[0], last_bias[1]], axis=1), last_bias[2]], axis=1)
    bias_share = sum(bias_shares) + bias_share
    out_bias_share = jnp.pad(sum(out_bias_shares) + out_bias_grad, ((0, 0), (0, features - width)))
    shares = jnp.concatenate([bias_share, out_bias_share])
    shares = shares + swapped(shares, "dp", 1)
    block, kept, paired, arrived, shares = together(block, kept, paired, arrived, shares)
    fired, act_total = counts[0], counts[1:]
    penalty = penalty_scale * act_total
    shares = rest_of(shares)
    arrived.append(crossed(2, block))
    enc_bias_grad, dec_bias_grad = shares[0], shares[1, :width]
    first_dp = dp_at == 0
    first_both = first_dp & (feat_at == 0)
    bias_squares = jnp.where(first_dp, jnp.sum(enc_bias_grad * enc_bias_grad), 0.0)
    bias_squares = bias_squares + jnp.where(first_both, jnp.sum(dec_bias_grad * dec_bias_grad), 0.0)
    row = lax.broadcasted_iota(jnp.int32, (16, LANES), 0)
    column = lax.broadcasted_iota(jnp.int32, (16, LANES), 1)
    norms = jnp.where((row == 0) & (column == 0), bias_squares, 0.0)
    norms = norms + jnp.where((row == 8) & (column == 0), loss_share, 0.0)
    norms = norms + jnp.pad(fit_part, ((8, 0), (0, 0)))
    for part in range(LAST_PARTS):
        *grads, part_norms = finished(kept[part], paired[part], arrived[part], penalty, both, grads, part)
        norms = norms + part_norms

    norms = summed(norms, everywhere)
    loss_total = jnp.sum(norms[8:])
    overall_derivative_length = jnp.sqrt(jnp.sum(norms[:8]))
    factor = jnp.minimum(1.0, CLIP_NORM / (overall_derivative_length + 1e-06))
    dec_new, dec_m, dec_v = adamw(dec_weight.T, grads[1] * factor, dec_weight_m.T, dec_weight_v.T, DECAY)
    dec_new, dec_m, dec_v = together(dec_new, dec_m, dec_v)
    row_squares = jnp.sum(dec_new * dec_new, axis=0, keepdims=True)
    row_squares = row_squares + swapped(row_squares, "dp", 1)
    enc_grad, row_squares = together(grads[0], row_squares)
    row_squares = rest_of(row_squares)
    enc_new, enc_m, enc_v = adamw(enc_weight, enc_grad * factor, enc_weight_m, enc_weight_v, DECAY)
    bias_new, bias_m, bias_v = adamw(enc_bias, enc_bias_grad * factor, enc_bias_m, enc_bias_v, 0.0)
    out_new, out_m, out_v = adamw(dec_bias, dec_bias_grad * factor, dec_bias_m, dec_bias_v, 0.0)
    dec_new = (dec_new * lax.rsqrt(row_squares + 1e-12)).T
    dec_m, dec_v = dec_m.T, dec_v.T
    return (
        jnp.stack([loss_total, counted[0, 0]]),
        overall_derivative_length,
        fired,
        enc_new,
        enc_m,
        enc_v,
        bias_new,
        bias_m,
        bias_v,
        dec_new,
        dec_m,
        dec_v,
        out_new,
        out_m,
        out_v,
    )


def solution(mesh):
    return jax.shard_map(
        shards,
        mesh=mesh,
        in_specs=(
            P(("dp", "feat"), None),
            P("dp", None),
            P("dp"),
            P(),
            P(),
            P(),
            P(),
            P("dp", "feat"),
            P("feat"),
            P("feat", "dp"),
            P(),
            P("dp", "feat"),
            P("dp", "feat"),
            P("feat"),
            P("feat"),
            P("feat", "dp"),
            P("feat", "dp"),
            P(),
            P(),
        ),
        out_specs=(
            P(),
            P(),
            P("feat"),
            P("dp", "feat"),
            P("dp", "feat"),
            P("dp", "feat"),
            P("feat"),
            P("feat"),
            P("feat"),
            P("feat", "dp"),
            P("feat", "dp"),
            P("feat", "dp"),
            P(),
            P(),
            P(),
        ),
        check_vma=False,
    )
```
